128 devices in a mesh: grp: 4 (over x), seq: 32 (over y, z, core).
Axes of the slice: x: 4, y: 4, z: 4, core: 2. Of those that a mesh axis runs over, the one named last changes fastest.
Arguments:
- compressed: bfloat16 [524288, 576], P(('grp', 'seq')), may hold values from -6 to 6
- block_channel_scale: float32 [4096, 576], P(('grp', 'seq')), may hold values from 0.2 to 2.5
- outlier_channels: int32 [4096, 16], P(('grp', 'seq')), may hold values from 0 to 575, all different within a row
- outlier_values: bfloat16 [4096, 16, 128], P(('grp', 'seq')), may hold values from -16 to 16
- lengths: int32 [4, 4], replicated, may hold values from 1 to 12, 32 in all within a row
- assignment: int32 [4, 4], replicated, may hold values from 0 to 3, each once within a row
- padding: int32 [4, 4], replicated, may hold values from 0 to 127
- queries: bfloat16 [16, 512, 576], P('grp')
- decode_token_latent: bfloat16 [16, 4, 576], P('grp'), may hold values from -8 to 8
Outputs:
- decode_cache: bfloat16 [4, 4, 32, 12, 128, 576], P('grp', None, 'seq')
- attended: bfloat16 [16, 512, 512], P('grp', 'seq')
The draws below stay inside these ranges and needn't reach their ends.
Inputs may be any that keep to these rules, and one draw needn't show every extreme that they name: `lengths`: each row sums to 32, and its largest entry is exactly 12. `assignment`: each row is a permutation: every prefill group sends one request to each decode group. `outlier_channels`: the 16 channels of a block are distinct.
All inputs are finite; a program needn't handle non-finite values.
Results may differ from the reference program's by a relative error of at most 0.0087.
The reference program's roundings to bfloat16 on the way (of `latent` and `weights`) count: a program that leaves them out, or rounds other values in their place, can miss the bound.
Values may be sent and summed in bfloat16 or wider, within the bound.
No kernel may reach another device: no remote copies, remote signals or barrier semaphores. Data moves between devices by JAX's collectives and lax.ppermute only.
A program may use at most 128 MiB of HBM per device.

```python
import math
import jax
import jax.numpy as jnp
import numpy as np
from jax import lax

LATENT_CHANNELS = 512
HEADS = 128
STEPS = 4
BLOCK = 128
OUTLIERS = 16
BLOCKS_DEV = 32
CHANNELS = 576
MOST_STRIPES = 12
QUERY_ROWS = 512
SLOTS = 16
BLOCKS_ALL = 4096
TOKENS = 524288
N_GRP = 4
N_SEQ = 32


def draw_queries(key, part):
    key = jax.random.fold_in(key, 11)
    first, second = jax.random.split(key, 2)
    shape = (SLOTS, QUERY_ROWS, CHANNELS)
    row_scale = jnp.exp(jax.random.uniform(second, (SLOTS, QUERY_ROWS, 1), jnp.float32, -0.7, 0.7))
    base = jax.random.normal(first, shape, jnp.float32) * row_scale
    return base.astype(jnp.bfloat16)


def touch_ends(entries, stream_key, smallest, largest):
    longest = entries.shape.index(max(entries.shape))
    spots = []
    for shift in (0, 1):
        where = [jax.random.randint(jax.random.fold_in(stream_key, axis), (), 0, length) for axis, length in enumerate(entries.shape)]
        where[longest] = (where[longest] + shift) % entries.shape[longest]
        spots.append(tuple(where))
    return entries.at[spots[0]].set(smallest).at[spots[1]].set(largest)


def block_levels(key, extent, cuts, smallest, top_value):
    factor_of = 1.0
    for axis_at, shards_of in cuts:
        draws = jax.random.uniform(jax.random.fold_in(jax.random.fold_in(key, 6), axis_at), (shards_of,), jnp.float32, smallest / len(cuts), top_value / len(cuts))
        factor_of = factor_of * jnp.repeat(jnp.exp(draws), extent[axis_at] // shards_of).reshape((-1,) + (1,) * (len(extent) - 1 - axis_at))
    return factor_of


def different_ones(own_key, rows, count, top, lift):
    sequence = jax.random.permutation(jax.random.fold_in(own_key, 1), count)
    favour = sequence
    for power in range(3):
        favour = favour * favour // count
    favour = favour * lift // count
    tickets = jax.random.randint(jax.random.fold_in(own_key, 2), (rows, count), 0, 4096) + favour
    holders = jax.random.permutation(jax.random.fold_in(own_key, 3), rows)[jnp.arange(count) % rows]
    tickets = jnp.where(jnp.arange(rows)[:, None] == holders[None, :], 1 << 14, tickets)
    score = tickets * count + jnp.arange(count)
    return lax.top_k(score.astype(jnp.int32), top)[1].astype(jnp.int32)


def split_up(number_of, total, reach, lean):
    weights = [(1 << 20) // math.isqrt(rank ** lean) + 1 for rank in range(2, number_of + 1)]
    surplus, given = total - reach - (number_of - 1), [1] * (number_of - 1)
    while surplus > 0:
        free = [i for i in range(number_of - 1) if given[i] < reach]
        whole, budget = sum([weights[i] for i in free]), surplus
        for i in free:
            more = min(reach - given[i], max(1, budget * weights[i] // whole), surplus)
            given[i] = given[i] + more
            surplus = surplus - more
    return np.array([reach] + given)


def uneven_parts(rng, number_of, total, most, slope):
    if number_of == 2:
        one = jax.random.randint(rng, (), max(1, total - most), min(most, total - 1) + 1)
        return jnp.stack([one, total - one])
    sizes = jnp.asarray(split_up(number_of, total, most, slope), jnp.int32)
    twos = (number_of - 1) // 2
    source_of, sink = sizes[1:1 + 2 * twos:2], sizes[2:2 + 2 * twos:2]
    slack = jnp.minimum(source_of - 1, most - sink)
    moved = jax.random.randint(jax.random.fold_in(rng, 1), (twos,), 0, 1 << 20) % (slack + 1)
    sizes = sizes.at[1:1 + 2 * twos:2].set(source_of - moved).at[2:2 + 2 * twos:2].set(sink + moved)
    return sizes[jax.random.permutation(jax.random.fold_in(rng, 2), number_of)]


def centred(rng, extent, scale, most, pieces=(), kind=jnp.bfloat16):
    drawn = jax.random.normal(rng, extent, jnp.float32) * scale
    if len(pieces) > 0:
        drawn = block_levels(rng, extent, pieces, -0.22, 0.18) * drawn
    return jnp.clip(drawn, min=-most, max=most).astype(kind)


def setup_inputs(seed: int = 0) -> dict:
    key_list = jax.random.split(jax.random.key(seed), 10)
    return {
        "compressed": centred(key_list[0], (TOKENS, CHANNELS), 1.0, 6.0, ((0, 128),)),
        "block_channel_scale": jnp.clip(jnp.exp(math.log(2.5) - 2.5257286 * jax.random.uniform(key_list[1], (BLOCKS_ALL, CHANNELS), jnp.float32) ** block_levels(key_list[1], (BLOCKS_ALL, CHANNELS), ((0, 128),), -0.2, 0.2)), 0.2, 2.5),
        "outlier_channels": different_ones(key_list[2], BLOCKS_ALL, CHANNELS, OUTLIERS, 0),
        "outlier_values": centred(key_list[3], (BLOCKS_ALL, OUTLIERS, BLOCK), 3.0, 16.0, ((0, 128),)),
        "lengths": jax.vmap(lambda own: uneven_parts(own, N_GRP, BLOCKS_DEV, MOST_STRIPES, 2))(jax.random.split(key_list[4], N_GRP)).reshape((N_GRP, N_GRP)).astype(jnp.int32),
        "assignment": jax.vmap(lambda own: jax.random.permutation(own, N_GRP))(jax.random.split(key_list[5], N_GRP)).reshape((N_GRP, N_GRP)).astype(jnp.int32),
        "padding": touch_ends(jax.random.randint(key_list[6], (N_GRP, N_GRP), 0, BLOCK), jax.random.fold_in(key_list[6], 1), 0, BLOCK - 1).astype(jnp.int32),
        "queries": draw_queries(jax.random.fold_in(key_list[9], 71), 0),
        "decode_token_latent": centred(key_list[8], (SLOTS, STEPS, CHANNELS), 1.5, 8.0, ((0, 4),)),
    }


NEG_FILL = -1.0e30
SCORE_SCALE = 192.0 ** -0.5


def dequantize(compressed, block_channel_scale, outlier_channels, outlier_values):
    blocks, channels = block_channel_scale.shape
    channel_ids = jnp.arange(channels, dtype=jnp.int32)
    onehot = (outlier_channels[:, :, None] == channel_ids[None, None, :]).astype(jnp.float32)
    plain_mask = 1.0 - jnp.sum(onehot, axis=1)
    scaled = compressed.reshape(blocks, -1, channels).astype(jnp.float32) * (block_channel_scale * plain_mask)[:, None, :]
    outliers = jnp.einsum("bkt,bkc->btc", outlier_values.astype(jnp.float32), onehot, precision=lax.Precision.HIGHEST)
    return (scaled + outliers).astype(jnp.bfloat16)


def slot_tables(lengths, assignment, padding, seq_count, rows_per_block):
    groups = lengths.shape[0]
    target = jnp.arange(groups, dtype=jnp.int32)
    matched = assignment[None, :, :] == target[:, None, None]
    offsets = jnp.cumsum(lengths, axis=1) - lengths

    def per_slot(values_table):
        return jnp.sum(jnp.where(matched, values_table[None, :, :], 0), axis=2).astype(jnp.int32)

    slot_len = per_slot(lengths)
    slot_off = per_slot(offsets)
    slot_live = slot_len * (seq_count * rows_per_block) - per_slot(padding)
    return slot_len, slot_off, slot_live


def attend_slot(cache_keys, live_mask, queries, decode_token_latent):
    scores = jnp.dot(queries, cache_keys.T, preferred_element_type=jnp.float32) * SCORE_SCALE
    scores = jnp.where(live_mask[None, :], scores, NEG_FILL)
    new_scores = jnp.dot(queries, decode_token_latent.T, preferred_element_type=jnp.float32) * SCORE_SCALE
    row_step = jnp.arange(QUERY_ROWS, dtype=jnp.int32) // HEADS
    col_step = jnp.arange(STEPS, dtype=jnp.int32)
    new_scores = jnp.where(col_step[None, :] <= row_step[:, None], new_scores, NEG_FILL)
    row_max = jnp.maximum(jnp.max(scores, axis=1), jnp.max(new_scores, axis=1))
    weights = jnp.exp(scores - row_max[:, None]).astype(jnp.bfloat16)
    fresh_weights = jnp.exp(new_scores - row_max[:, None]).astype(jnp.bfloat16)
    weighted_values = jnp.dot(weights, cache_keys[:, :LATENT_CHANNELS], preferred_element_type=jnp.float32)
    weighted_values = weighted_values + jnp.dot(fresh_weights, decode_token_latent[:, :LATENT_CHANNELS], preferred_element_type=jnp.float32)
    weight_total_sum = jnp.sum(weights.astype(jnp.float32), axis=1) + jnp.sum(fresh_weights.astype(jnp.float32), axis=1)
    return (weighted_values / weight_total_sum[:, None]).astype(jnp.bfloat16)


def attend_bundle(bundle):
    return attend_slot(bundle[0], bundle[1], bundle[2], bundle[3])


def reference(compressed, block_channel_scale, outlier_channels, outlier_values, lengths, assignment, padding, queries, decode_token_latent):
    latent = dequantize(compressed, block_channel_scale, outlier_channels, outlier_values)
    latent = latent.reshape(N_GRP, BLOCKS_DEV, N_SEQ, BLOCK, CHANNELS)
    slot_len, slot_off, slot_live = slot_tables(lengths, assignment, padding, N_SEQ, BLOCK)
    stripe_ids = jnp.arange(MOST_STRIPES, dtype=jnp.int32)
    source = jnp.clip(slot_off[:, :, None] + stripe_ids[None, None, :], 0, BLOCKS_DEV - 1)
    group_ids = jnp.broadcast_to(jnp.arange(N_GRP, dtype=jnp.int32)[None, :, None], source.shape)
    gathered = latent[group_ids, source]
    gathered = jnp.transpose(gathered, (0, 1, 3, 2, 4, 5))
    seq_ids = jnp.arange(N_SEQ, dtype=jnp.int32)
    token_ids = jnp.arange(BLOCK, dtype=jnp.int32)
    position = (stripe_ids[None, :, None] * N_SEQ + seq_ids[:, None, None]) * BLOCK + token_ids[None, None, :]
    live_mask = position[None, None] < slot_live[:, :, None, None, None]
    decode_cache = jnp.where(live_mask[..., None], gathered, jnp.zeros((), jnp.bfloat16))
    flat_cache = decode_cache.reshape(SLOTS, -1, CHANNELS)
    flat_mask = live_mask.reshape(SLOTS, -1)
    attended = lax.map(attend_bundle, (flat_cache, flat_mask, queries, decode_token_latent))
    return decode_cache, attended
```

```python
import functools

import jax
import jax.numpy as jnp
from jax import lax
from jax.experimental import pallas as pl
from jax.experimental.pallas import tpu as pltpu
from jax.sharding import PartitionSpec as P

LATENT_CHANNELS = 512
MOST_STRIPES = 12
HEADS = 128
NEG_FILL = -1e30
SCORE_SCALE = 192.0 ** (-0.5)
CHUNKS = (144, 144, 144, 144)
KEY_TILE = 8
NOTE_LANES = 128

SMEM = pl.BlockSpec(memory_space=pltpu.SMEM)
ANY = pl.BlockSpec(memory_space=pl.ANY)
VMEM = pl.BlockSpec(memory_space=pltpu.VMEM)


def params(**more):
    return pltpu.CompilerParams(vmem_limit_bytes=48 << 20, **more)


def request_for(lengths, assignment, group, target):
    first, count, before = 0, 0, 0
    for r in range(4):
        here = lengths[group, r]
        hit = assignment[group, r] == target
        first = jnp.where(hit, before, first)
        count = jnp.where(hit, here, count)
        before = before + here
    return first, count


def request_of(lengths, assignment, padding, group, stripe):
    target, empty, before = 0, 0, 0
    for r in range(4):
        after = before + lengths[group, r]
        inside = jnp.logical_and(stripe >= before, stripe < after)
        target = jnp.where(inside, assignment[group, r], target)
        empty = jnp.where(stripe == after - 1, padding[group, r], empty)
        before = after
    return target, empty


def dequantize_kernel(start, per_step, total, place, lengths, assignment, padding, packed, scale, channels, values, out):
    rows = packed.shape[0]
    step = pl.program_id(0)
    _, empty = request_of(lengths, assignment, padding, place[0], place[1])
    ids = lax.broadcasted_iota(jnp.int32, (rows, 16), 0) + start
    ones = jnp.ones((16, 128), jnp.bfloat16)
    tokens = lax.broadcasted_iota(jnp.int32, (rows, 128), 1)
    for b in range(per_step):
        onehot = (ids == channels[b : b + 1, :]).astype(jnp.bfloat16)
        spread = jnp.dot(
            onehot, jnp.concatenate([values[b], ones], axis=1), preferred_element_type=jnp.float32
        )
        plain = packed[:, b * 128 : (b + 1) * 128].astype(jnp.float32) * scale[0, :, b : b + 1]
        latent = jnp.where(spread[:, 128:] > 0.5, spread[:, :128], plain)
        if b == per_step - 1:
            limit = jnp.where(step == total - 1, 128 - empty, 128)
            latent = jnp.where(tokens < limit, latent, 0.0)
        out[b] = latent.astype(jnp.bfloat16)


def dequantize(start, rows, place, lengths, assignment, padding, packed, scale, channels, values):
    blocks = channels.shape[0]
    per_step = 8
    steps = blocks // per_step
    assert start % rows == 0
    return pl.pallas_call(
        functools.partial(dequantize_kernel, start, per_step, steps),
        grid=(steps,),
        out_shape=jax.ShapeDtypeStruct((blocks, rows, 128), jnp.bfloat16),
        in_specs=[
            SMEM,
            SMEM,
            SMEM,
            SMEM,
            pl.BlockSpec((rows, per_step * 128), lambda i: (start // rows, i)),
            pl.BlockSpec((1, rows, per_step), lambda i: (i, start // rows, 0)),
            pl.BlockSpec((per_step, 16), lambda i: (i, 0)),
            pl.BlockSpec((per_step, 16, 128), lambda i: (i, 0, 0)),
        ],
        out_specs=pl.BlockSpec((per_step, rows, 128), lambda i: (i, 0, 0)),
        compiler_params=params(),
        cost_estimate=pl.CostEstimate(
            flops=4 * blocks * rows * 128, bytes_accessed=4 * blocks * rows * 128, transcendentals=0
        ),
        name="dequantize",
    )(place, lengths, assignment, padding, packed, scale, channels, values)


def start_request(first, count, stripes, target, zeros, sem):
    for v in range(MOST_STRIPES):

        @pl.when(v < count)
        def _():
            pltpu.make_async_copy(stripes.at[first + v], target(v), sem).start()

        @pl.when(v >= count)
        def _():
            pltpu.make_async_copy(zeros, target(v), sem).start()


def pack_kernel(place, lengths, assignment, stripes, out1, out2, out3, zeros, sems):
    zeros[...] = jnp.zeros_like(zeros)
    outs = (out1, out2, out3)
    for d in (1, 2, 3):
        first, count = request_for(lengths, assignment, place[0], lax.rem(place[0] + d, 4))
        start_request(first, count, stripes, lambda v, o=outs[d - 1]: o.at[v], zeros, sems.at[d - 1])
    for d in (1, 2, 3):
        pltpu.make_async_copy(outs[d - 1], outs[d - 1], sems.at[d - 1]).wait()


def pack(place, lengths, assignment, stripes):
    rows = stripes.shape[1]
    one = jax.ShapeDtypeStruct((MOST_STRIPES, rows, 128), jnp.bfloat16)
    return pl.pallas_call(
        pack_kernel,
        out_shape=(one, one, one),
        in_specs=[SMEM, SMEM, SMEM, ANY],
        out_specs=(ANY, ANY, ANY),
        scratch_shapes=[pltpu.VMEM((rows, 128), jnp.bfloat16), pltpu.SemaphoreType.DMA((3,))],
        compiler_params=params(),
        cost_estimate=pl.CostEstimate(flops=0, bytes_accessed=4 * 36 * rows * 128, transcendentals=0),
        name="pack",
    )(place, lengths, assignment, stripes)


def place_kernel(start, first_chunk, *refs):
    if first_chunk:
        place, lengths, assignment, stripes, in1, in2, in3, out, zeros, sems = refs
    else:
        place, lengths, assignment, stripes, in1, in2, in3, _, out, zeros, sems = refs
    rows = stripes.shape[1]
    zeros[...] = jnp.zeros_like(zeros)
    here = place[0]

    def slot(d):
        return out.at[lax.rem(here + 4 - d, 4), :, pl.ds(start, rows), :]

    copies = [pltpu.make_async_copy(x, slot(d), sems.at[d]) for d, x in ((1, in1), (2, in2), (3, in3))]
    for copy in copies:
        copy.start()
    first, count = request_for(lengths, assignment, here, here)
    start_request(first, count, stripes, lambda v: out.at[here, v, pl.ds(start, rows), :], zeros, sems.at[0])
    for copy in copies:
        copy.wait()
    pltpu.make_async_copy(slot(0), slot(0), sems.at[0]).wait()


def put(start, place, lengths, assignment, stripes, arrived, cache):
    rows = stripes.shape[1]
    more = () if cache is None else (cache,)
    return pl.pallas_call(
        functools.partial(place_kernel, start, cache is None),
        out_shape=jax.ShapeDtypeStruct((4, MOST_STRIPES, sum(CHUNKS), 128), jnp.bfloat16),
        in_specs=[SMEM, SMEM, SMEM, ANY, ANY, ANY, ANY] + [ANY] * len(more),
        out_specs=ANY,
        input_output_aliases={7: 0} if more else {},
        scratch_shapes=[pltpu.VMEM((rows, 128), jnp.bfloat16), pltpu.SemaphoreType.DMA((4,))],
        compiler_params=params(),
        cost_estimate=pl.CostEstimate(flops=0, bytes_accessed=4 * 48 * rows * 128, transcendentals=0),
        name="put",
    )(place, lengths, assignment, stripes, *arrived, *more)


def pick_kernel(place, lengths, assignment, padding, pieces, out):
    for s in range(32):
        target, _ = request_of(lengths, assignment, padding, place[0], s)
        out[s] = pieces[target]


def pick(place, lengths, assignment, padding, pieces):
    return pl.pallas_call(
        pick_kernel,
        out_shape=jax.ShapeDtypeStruct((32,) + pieces.shape[1:], pieces.dtype),
        in_specs=[SMEM, SMEM, SMEM, SMEM, VMEM],
        out_specs=VMEM,
        compiler_params=params(),
        name="pick",
    )(place, lengths, assignment, padding, pieces)


def in_three(x):
    high = x.astype(jnp.bfloat16)
    rest = x - high.astype(jnp.float32)
    middle = rest.astype(jnp.bfloat16)
    low = (rest - middle.astype(jnp.float32)).astype(jnp.bfloat16)
    return high, middle, low


def attend_kernel(steps, place, lengths, assignment, padding, queries, *refs):
    keys, (out, peak, total, weighted) = refs[: len(CHUNKS)], refs[len(CHUNKS) :]
    step = pl.program_id(0)
    _, empty = request_of(lengths, assignment, padding, place[0], place[1])

    @pl.when(step == 0)
    def _():
        peak[...] = jnp.full_like(peak, NEG_FILL)
        total[...] = jnp.zeros_like(total)
        weighted[...] = jnp.zeros_like(weighted)

    latent = jnp.concatenate(
        [jnp.concatenate([k[b] for k in keys], axis=0) for b in range(KEY_TILE)], axis=1
    )
    scores = jnp.dot(queries[...], latent, preferred_element_type=jnp.float32) * SCORE_SCALE
    columns = lax.broadcasted_iota(jnp.int32, scores.shape, 1)
    limit = jnp.where(step == steps - 1, KEY_TILE * 128 - empty, KEY_TILE * 128)
    scores = jnp.where(columns < limit, scores, NEG_FILL)
    before = peak[...]
    now = jnp.maximum(before, jnp.max(scores, axis=1, keepdims=True))
    shrink = jnp.exp(before - now)
    weights = jnp.exp(scores - now[:, :1]).astype(jnp.bfloat16)
    total[...] = total[...] * shrink + jnp.sum(weights.astype(jnp.float32), axis=1, keepdims=True)
    weighted[...] = weighted[...] * shrink[:, :1] + lax.dot_general(
        weights, latent[:LATENT_CHANNELS], (((1,), (1,)), ((), ())), preferred_element_type=jnp.float32
    )
    peak[...] = now

    @pl.when(step == steps - 1)
    def _():
        out[:, :LATENT_CHANNELS] = weighted[...].astype(jnp.bfloat16)
        lane = lax.broadcasted_iota(jnp.int32, peak.shape, 1)
        note = jnp.zeros(peak.shape, jnp.float32)
        for i, part in enumerate(in_three(peak[...]) + in_three(total[...])):
            note = jnp.where(lane == i, part.astype(jnp.float32), note)
        out[:, LATENT_CHANNELS:] = note.astype(jnp.bfloat16)


def attend(place, lengths, assignment, padding, queries, keys):
    rows = queries.shape[0]
    blocks = keys[0].shape[0]
    steps = blocks // KEY_TILE
    width = LATENT_CHANNELS + NOTE_LANES
    return pl.pallas_call(
        functools.partial(attend_kernel, steps),
        grid=(steps,),
        out_shape=jax.ShapeDtypeStruct((rows, width), jnp.bfloat16),
        in_specs=[SMEM, SMEM, SMEM, SMEM, pl.BlockSpec(queries.shape, lambda i: (0, 0))]
        + [pl.BlockSpec((KEY_TILE,) + k.shape[1:], lambda i: (i, 0, 0)) for k in keys],
        out_specs=pl.BlockSpec((rows, width), lambda i: (0, 0)),
        scratch_shapes=[
            pltpu.VMEM((rows, 128), jnp.float32),
            pltpu.VMEM((rows, 128), jnp.float32),
            pltpu.VMEM((rows, LATENT_CHANNELS), jnp.float32),
        ],
        compiler_params=params(),
        cost_estimate=pl.CostEstimate(
            flops=2 * rows * blocks * 128 * (576 + 512), bytes_accessed=6 << 20, transcendentals=rows * blocks * 128
        ),
        name="attend",
    )(place, lengths, assignment, padding, queries, *keys)


def join_kernel(place, lengths, assignment, padding, partials, out):
    stripes, rows, _ = partials.shape
    note = partials[:, :, LATENT_CHANNELS:].astype(jnp.float32)
    peak = note[:, :, 0:1] + note[:, :, 1:2] + note[:, :, 2:3]
    total = note[:, :, 3:4] + note[:, :, 4:5] + note[:, :, 5:6]
    stripe = lax.broadcasted_iota(jnp.int32, peak.shape, 0)
    lane = lax.broadcasted_iota(jnp.int32, (rows, NOTE_LANES), 1)
    values = partials[:, :, :LATENT_CHANNELS].astype(jnp.float32)
    for target in range(4):
        first, count = request_for(lengths, assignment, place[0], target)
        inside = jnp.logical_and(stripe >= first, stripe < first + count)
        top = jnp.max(jnp.where(inside, peak, NEG_FILL), axis=0)
        factor = jnp.where(inside, jnp.exp(jnp.where(inside, peak, NEG_FILL) - top[None]), 0.0)
        out[target, :, :LATENT_CHANNELS] = jnp.sum(values * factor, axis=0)
        whole = jnp.sum(total * factor, axis=0)
        out[target, :, LATENT_CHANNELS:] = jnp.where(lane == 0, top, jnp.where(lane == 1, whole, 0.0))


def join(place, lengths, assignment, padding, partials):
    return pl.pallas_call(
        join_kernel,
        out_shape=jax.ShapeDtypeStruct((4,) + partials.shape[1:], jnp.float32),
        in_specs=[SMEM, SMEM, SMEM, SMEM, VMEM],
        out_specs=VMEM,
        compiler_params=params(),
        name="join",
    )(place, lengths, assignment, padding, partials)


def finish(joined, queries, fresh, seq_here):
    own = joined.shape[1]
    row_start = seq_here * own
    own_queries = lax.dynamic_slice_in_dim(queries, row_start, own, 1)
    scores = (
        jnp.einsum("yeu,ynu->yen", own_queries, fresh, preferred_element_type=jnp.float32) * SCORE_SCALE
    )
    row_step = (row_start + jnp.arange(own, dtype=jnp.int32)) // HEADS
    col_step = jnp.arange(fresh.shape[1], dtype=jnp.int32)
    scores = jnp.where((col_step[None, :] <= row_step[:, None])[None], scores, NEG_FILL)
    cache_peak = joined[:, :, LATENT_CHANNELS]
    cache_total = joined[:, :, LATENT_CHANNELS + 1]
    peak = jnp.maximum(cache_peak, jnp.max(scores, axis=2))
    shrink = jnp.exp(cache_peak - peak)
    weights = jnp.exp(scores - peak[:, :, None]).astype(jnp.bfloat16)
    weighted = joined[:, :, :LATENT_CHANNELS] * shrink[:, :, None] + jnp.einsum(
        "oep,opf->oef", weights, fresh[:, :, :LATENT_CHANNELS], preferred_element_type=jnp.float32
    )
    total = cache_total * shrink + jnp.sum(weights.astype(jnp.float32), axis=2)
    return (weighted / total[:, :, None]).astype(jnp.bfloat16)


def local(
    compressed,
    block_channel_scale,
    outlier_channels,
    outlier_values,
    lengths,
    assignment,
    padding,
    queries,
    decode_token_latent,
):
    group_here = lax.axis_index("grp")
    seq_here = lax.axis_index("seq")
    place = jnp.stack([group_here, seq_here]).astype(jnp.int32)
    packed = compressed.T
    scale = block_channel_scale.reshape(4, 8, -1).transpose(0, 2, 1)

    turned = queries.transpose(0, 2, 1)
    piece = lax.dynamic_slice(
        turned, (0, (seq_here // 4) * 72, (seq_here % 4) * 128), (4, 72, 128)
    )
    pieces = lax.all_to_all(piece, "grp", split_axis=0, concat_axis=0, tiled=True)
    picked = pick(place, lengths, assignment, padding, pieces)
    gathered = lax.all_to_all(picked, "seq", split_axis=0, concat_axis=0, tiled=True)
    own_queries = gathered.reshape(8, 4, 72, 128).transpose(1, 3, 0, 2).reshape(512, 576)

    starts = [sum(CHUNKS[:i]) for i in range(len(CHUNKS))]
    latent = [
        dequantize(
            start, rows, place, lengths, assignment, padding, packed, scale, outlier_channels, outlier_values
        )
        for start, rows in zip(starts, CHUNKS)
    ]
    cache = None
    for start, chunk in zip(starts, latent):
        stripes = lax.all_to_all(chunk, "seq", split_axis=0, concat_axis=0, tiled=True)
        outgoing = pack(place, lengths, assignment, stripes)
        arrived = [
            lax.ppermute(x, "grp", [(i, (i + d) % 4) for i in range(4)]) for d, x in zip((1, 2, 3), outgoing)
        ]
        cache = put(start, place, lengths, assignment, stripes, arrived, cache)

    partial = attend(place, lengths, assignment, padding, own_queries, latent)
    partials = lax.all_to_all(
        partial.reshape(32, 16, partial.shape[1]), "seq", split_axis=0, concat_axis=0, tiled=True
    )
    joined = lax.all_to_all(
        join(place, lengths, assignment, padding, partials), "grp", split_axis=0, concat_axis=0, tiled=True
    )
    attended = finish(joined, queries, decode_token_latent, seq_here)
    return cache.transpose(0, 1, 3, 2)[None, :, None], attended


def solution(mesh):
    placed = (
        P(("grp", "seq"), None),
        P(("grp", "seq"), None),
        P(("grp", "seq"), None),
        P(("grp", "seq"), None, None),
        P(),
        P(),
        P(),
        P("grp", None, None),
        P("grp", None, None),
    )
    return jax.shard_map(
        local,
        mesh=mesh,
        in_specs=placed,
        out_specs=(P("grp", None, "seq", None, None, None), P("grp", "seq", None)),
        check_vma=False,
    )
```

```python
import functools

import jax
import jax.numpy as jnp
from jax import lax
from jax.experimental import pallas as pl
from jax.experimental.pallas import tpu as pltpu
from jax.sharding import PartitionSpec as P

LATENT_CHANNELS = 512
MOST_STRIPES = 12
HEADS = 128
NEG_FILL = -1e30
SCORE_SCALE = 192.0 ** (-0.5)
CHUNKS = (336, 240)
KEY_TILE = 8
NOTE_LANES = 128

SMEM = pl.BlockSpec(memory_space=pltpu.SMEM)
HBM = pl.BlockSpec(memory_space=pltpu.HBM)
VMEM = pl.BlockSpec(memory_space=pltpu.VMEM)


def params(megabytes=16):
    return pltpu.CompilerParams(vmem_limit_bytes=megabytes << 20)


def moved(steps, rows):
    size = 2 * steps * MOST_STRIPES * rows * 128
    return pl.CostEstimate(flops=0, bytes_accessed=2 * size, transcendentals=0)


def request_for(table, target):
    first, count, before = 0, 0, 0
    for r in range(4):
        here = table[2 + r]
        hit = table[6 + r] == target
        first = jnp.where(hit, before, first)
        count = jnp.where(hit, here, count)
        before = before + here
    return first, count


def request_here(table):
    target, empty, before = 0, 0, 0
    for r in range(4):
        after = before + table[2 + r]
        inside = jnp.logical_and(table[1] >= before, table[1] < after)
        target = jnp.where(inside, table[6 + r], target)
        empty = jnp.where(table[1] == after - 1, table[10 + r], empty)
        before = after
    return target, empty


def dequantize_kernel(start, per_step, total, table, packed, scale, channels, values, out, scales, marks):
    rows = packed.shape[0]
    width = per_step * 16
    step = pl.program_id(0)

    @pl.when(step == 0)
    def _():
        mark = channels[...].astype(jnp.float32).T
        ids = lax.broadcasted_iota(jnp.int32, scale.shape, 1).astype(jnp.float32)
        plain = scale[...]
        for k in range(16):
            plain = jnp.where(ids == mark[:, k : k + 1], 0.0, plain)
        turned = plain.T[start : start + rows]
        for i in range(total):
            scales[i] = turned[:, i * per_step : (i + 1) * per_step]
            marks[i] = jnp.concatenate([mark[i * per_step + b : i * per_step + b + 1] for b in range(per_step)], axis=1)

    _, empty = request_here(table)
    ids = (lax.broadcasted_iota(jnp.int32, (rows, width), 0) + start).astype(jnp.float32)
    onehot = (ids == marks[step]).astype(jnp.bfloat16)
    flat = values[...].reshape(width, 128)
    block = lax.broadcasted_iota(jnp.int32, (width, 128), 0) // 16
    spread = jnp.concatenate([jnp.where(block == b, flat, jnp.zeros_like(flat)) for b in range(per_step)], axis=1)
    outliers = jnp.dot(onehot, spread, preferred_element_type=jnp.float32)
    tokens = lax.broadcasted_iota(jnp.int32, (rows, 128), 1)
    here = scales[step]
    for b in range(per_step):
        lanes = slice(b * 128, (b + 1) * 128)
        latent = packed[:, lanes].astype(jnp.float32) * here[:, b : b + 1] + outliers[:, lanes]
        if b == per_step - 1:
            limit = jnp.where(step == total - 1, 128 - empty, 128)
            latent = jnp.where(tokens < limit, latent, 0.0)
        out[b] = latent.astype(jnp.bfloat16)


def dequantize(start, rows, table, packed, scale, channels, values):
    blocks = scale.shape[0]
    per_step = 8
    steps = blocks // per_step
    return pl.pallas_call(
        functools.partial(dequantize_kernel, start, per_step, steps),
        grid=(steps,),
        out_shape=pltpu.HBM((blocks, rows, 128), jnp.bfloat16),
        in_specs=[
            SMEM,
            pl.BlockSpec((pl.Element(rows), pl.Element(per_step * 128)), lambda i: (start, i * per_step * 128)),
            pl.BlockSpec(scale.shape, lambda i: (0, 0)),
            pl.BlockSpec(channels.shape, lambda i: (0, 0)),
            pl.BlockSpec((per_step, 16, 128), lambda i: (i, 0, 0)),
        ],
        out_specs=pl.BlockSpec((per_step, rows, 128), lambda i: (i, 0, 0)),
        scratch_shapes=[
            pltpu.VMEM((steps, rows, per_step), jnp.float32),
            pltpu.VMEM((steps, 1, per_step * 16), jnp.float32),
        ],
        compiler_params=params(60),
        cost_estimate=pl.CostEstimate(
            flops=4 * blocks * rows * 128, bytes_accessed=4 * blocks * rows * 128, transcendentals=0
        ),
        name="dequantize",
    )(table, packed, scale, channels, values)


def collect(table, steps, stripes, targets, zeros, sems):
    zeros[...] = jnp.zeros_like(zeros)
    for i, d in enumerate(steps):
        first, count = request_for(table, lax.rem(table[0] + d, 4))
        for v in range(MOST_STRIPES):

            @pl.when(v < count)
            def _():
                pltpu.make_async_copy(stripes.at[first + v], targets[i].at[v], sems.at[i]).start()

            @pl.when(v >= count)
            def _():
                pltpu.make_async_copy(zeros, targets[i].at[v], sems.at[i]).start()

    for i in range(len(steps)):
        pltpu.make_async_copy(targets[i], targets[i], sems.at[i]).wait()


def collect_scratch(steps, rows):
    return [pltpu.VMEM((rows, 128), jnp.bfloat16), pltpu.SemaphoreType.DMA((steps,))]


def pack_kernel(steps, table, stripes, *refs):
    outs, scratch = refs[: len(steps)], refs[len(steps) :]
    collect(table, steps, stripes, outs, *scratch)


def pack(table, stripes, steps):
    rows = stripes.shape[1]
    one = pltpu.HBM((MOST_STRIPES, rows, 128), jnp.bfloat16)
    return pl.pallas_call(
        functools.partial(pack_kernel, steps),
        out_shape=(one,) * len(steps),
        in_specs=[SMEM, VMEM],
        out_specs=(HBM,) * len(steps),
        scratch_shapes=collect_scratch(len(steps), rows),
        compiler_params=params(),
        cost_estimate=moved(len(steps), rows),
        name="pack",
    )(table, stripes)


def own_kernel(start, table, stripes, *refs):
    out, scratch = refs[-3], refs[-2:]
    rows = stripes.shape[1]
    collect(table, (0,), stripes, [out.at[table[0], :, pl.ds(start, rows), :]], *scratch)


def own(start, table, stripes, cache):
    rows = stripes.shape[1]
    more = () if cache is None else (cache,)
    return pl.pallas_call(
        functools.partial(own_kernel, start),
        out_shape=jax.ShapeDtypeStruct((4, MOST_STRIPES, sum(CHUNKS), 128), jnp.bfloat16),
        in_specs=[SMEM, VMEM] + [HBM] * len(more),
        out_specs=HBM,
        input_output_aliases={2: 0} if more else {},
        scratch_shapes=collect_scratch(1, rows),
        compiler_params=params(),
        cost_estimate=moved(1, rows),
        name="own",
    )(table, stripes, *more)


def put_kernel(start, steps, table, *refs):
    arrived, (_, out, sems) = refs[: len(steps)], refs[len(steps) :]
    rows = arrived[0].shape[1]
    copies = [
        pltpu.make_async_copy(
            arrived[i], out.at[lax.rem(table[0] + 4 - d, 4), :, pl.ds(start, rows), :], sems.at[i]
        )
        for i, d in enumerate(steps)
    ]
    for copy in copies:
        copy.start()
    for copy in copies:
        copy.wait()


def put(start, table, steps, arrived, cache):
    rows = arrived[0].shape[1]
    return pl.pallas_call(
        functools.partial(put_kernel, start, steps),
        out_shape=jax.ShapeDtypeStruct(cache.shape, cache.dtype),
        in_specs=[SMEM] + [VMEM] * len(steps) + [HBM],
        out_specs=HBM,
        input_output_aliases={len(steps) + 1: 0},
        scratch_shapes=[pltpu.SemaphoreType.DMA((len(steps),))],
        compiler_params=params(),
        cost_estimate=moved(len(steps), rows),
        name="put",
    )(table, *arrived, cache)


def split_kernel(table, queries, *refs):
    outs, (held, in_sems, out_sems) = refs[:3], refs[3:]
    come = [
        pltpu.make_async_copy(queries.at[lax.rem(table[0] + d + 1, 4)], held.at[d], in_sems.at[d]) for d in range(3)
    ]
    leave = [pltpu.make_async_copy(held.at[d], outs[d], out_sems.at[d]) for d in range(3)]
    for copy in come:
        copy.start()
    for d in range(3):
        come[d].wait()
        leave[d].start()
    for copy in leave:
        copy.wait()


def split(table, queries):
    one = pltpu.HBM(queries.shape[1:], queries.dtype)
    return pl.pallas_call(
        split_kernel,
        out_shape=(one,) * 3,
        in_specs=[SMEM, HBM],
        out_specs=(HBM,) * 3,
        scratch_shapes=[
            pltpu.VMEM((3,) + queries.shape[1:], queries.dtype),
            pltpu.SemaphoreType.DMA((3,)),
            pltpu.SemaphoreType.DMA((3,)),
        ],
        compiler_params=params(),
        name="split",
    )(table, pltpu.with_memory_space_constraint(queries, pltpu.HBM))


def in_three(x):
    high = x.astype(jnp.bfloat16)
    rest = x - high.astype(jnp.float32)
    middle = rest.astype(jnp.bfloat16)
    low = (rest - middle.astype(jnp.float32)).astype(jnp.bfloat16)
    return high, middle, low


def attend_kernel(steps, table, *refs):
    sources, keys = refs[:4], refs[4 : 4 + len(CHUNKS)]
    out, peak, total, weighted, turned, queries, sem = refs[4 + len(CHUNKS) :]
    step = pl.program_id(0)
    target, empty = request_here(table)

    @pl.when(step == 0)
    def _():
        for d in range(4):
            source = sources[d].at[table[0]] if d == 0 else sources[d]

            @pl.when(target == lax.rem(table[0] + 4 - d, 4))
            def _():
                pltpu.make_async_copy(source, turned, sem).start()

        pltpu.make_async_copy(sources[1], turned, sem).wait()
        queries[...] = turned[...].T
        peak[...] = jnp.full_like(peak, NEG_FILL)
        total[...] = jnp.zeros_like(total)
        weighted[...] = jnp.zeros_like(weighted)

    latent = jnp.concatenate(
        [jnp.concatenate([k[b] for k in keys], axis=0) for b in range(KEY_TILE)], axis=1
    )
    scores = jnp.dot(queries[...], latent, preferred_element_type=jnp.float32) * SCORE_SCALE
    columns = lax.broadcasted_iota(jnp.int32, scores.shape, 1)
    limit = jnp.where(step == steps - 1, KEY_TILE * 128 - empty, KEY_TILE * 128)
    scores = jnp.where(columns < limit, scores, NEG_FILL)
    before = peak[...]
    now = jnp.maximum(before, jnp.max(scores, axis=1, keepdims=True))
    shrink = jnp.exp(before - now)
    weights = jnp.exp(scores - now[:, :1]).astype(jnp.bfloat16)
    total[...] = total[...] * shrink + jnp.sum(weights.astype(jnp.float32), axis=1, keepdims=True)
    weighted[...] = weighted[...] * shrink[:, :1] + lax.dot_general(
        weights, latent[:LATENT_CHANNELS], (((1,), (1,)), ((), ())), preferred_element_type=jnp.float32
    )
    peak[...] = now

    @pl.when(step == steps - 1)
    def _():
        out[:, :LATENT_CHANNELS] = weighted[...].astype(jnp.bfloat16)
        lane = lax.broadcasted_iota(jnp.int32, peak.shape, 1)
        note = jnp.zeros(peak.shape, jnp.float32)
        for i, part in enumerate(in_three(peak[...]) + in_three(total[...])):
            note = jnp.where(lane == i, part.astype(jnp.float32), note)
        out[:, LATENT_CHANNELS:] = note.astype(jnp.bfloat16)


def attend(table, queries, pieces, keys):
    channels, rows = queries.shape[1:]
    queries, *pieces = [pltpu.with_memory_space_constraint(x, pltpu.HBM) for x in (queries, *pieces)]
    keys = [pltpu.with_memory_space_constraint(k, pltpu.HBM) for k in keys]
    blocks = keys[0].shape[0]
    steps = blocks // KEY_TILE
    width = LATENT_CHANNELS + NOTE_LANES
    return pl.pallas_call(
        functools.partial(attend_kernel, steps),
        grid=(steps,),
        out_shape=jax.ShapeDtypeStruct((rows, width), jnp.bfloat16),
        in_specs=[SMEM] + [HBM] * 4
        + [pl.BlockSpec((KEY_TILE,) + k.shape[1:], lambda i: (i, 0, 0)) for k in keys],
        out_specs=pl.BlockSpec((rows, width), lambda i: (0, 0)),
        scratch_shapes=[
            pltpu.VMEM((rows, 128), jnp.float32),
            pltpu.VMEM((rows, 128), jnp.float32),
            pltpu.VMEM((rows, LATENT_CHANNELS), jnp.float32),
            pltpu.VMEM((channels, rows), jnp.bfloat16),
            pltpu.VMEM((rows, channels), jnp.bfloat16),
            pltpu.SemaphoreType.DMA,
        ],
        compiler_params=params(40),
        cost_estimate=pl.CostEstimate(
            flops=16 * rows * blocks * 128 * (576 + 512), bytes_accessed=6 << 20, transcendentals=rows * blocks * 128
        ),
        name="attend",
    )(table, queries, *pieces, *keys)


def join_kernel(table, partials, out):
    stripes, rows, _ = partials.shape
    note = partials[:, :, LATENT_CHANNELS:].astype(jnp.float32)
    peak = note[:, :, 0:1] + note[:, :, 1:2] + note[:, :, 2:3]
    total = note[:, :, 3:4] + note[:, :, 4:5] + note[:, :, 5:6]
    stripe = lax.broadcasted_iota(jnp.int32, peak.shape, 0)
    lane = lax.broadcasted_iota(jnp.int32, (rows, NOTE_LANES), 1)
    values = partials[:, :, :LATENT_CHANNELS].astype(jnp.float32)
    for target in range(4):
        first, count = request_for(table, target)
        inside = jnp.logical_and(stripe >= first, stripe < first + count)
        top = jnp.max(jnp.where(inside, peak, NEG_FILL), axis=0)
        factor = jnp.where(inside, jnp.exp(jnp.where(inside, peak, NEG_FILL) - top[None]), 0.0)
        out[target, :, :LATENT_CHANNELS] = jnp.sum(values * factor, axis=0)
        whole = jnp.sum(total * factor, axis=0)
        out[target, :, LATENT_CHANNELS:] = jnp.where(lane == 0, top, jnp.where(lane == 1, whole, 0.0))


def join(table, partials):
    return pl.pallas_call(
        join_kernel,
        out_shape=jax.ShapeDtypeStruct((4,) + partials.shape[1:], jnp.float32),
        in_specs=[SMEM, VMEM],
        out_specs=VMEM,
        compiler_params=params(),
        name="join",
    )(table, partials)


def finish(joined, queries, fresh, seq_here):
    own = joined.shape[1]
    row_start = seq_here * own
    own_queries = lax.dynamic_slice_in_dim(queries, row_start, own, 1)
    scores = (
        jnp.einsum("yeu,ynu->yen", own_queries, fresh, preferred_element_type=jnp.float32) * SCORE_SCALE
    )
    row_step = (row_start + jnp.arange(own, dtype=jnp.int32)) // HEADS
    col_step = jnp.arange(fresh.shape[1], dtype=jnp.int32)
    scores = jnp.where((col_step[None, :] <= row_step[:, None])[None], scores, NEG_FILL)
    cache_peak = joined[:, :, LATENT_CHANNELS]
    cache_total = joined[:, :, LATENT_CHANNELS + 1]
    peak = jnp.maximum(cache_peak, jnp.max(scores, axis=2))
    shrink = jnp.exp(cache_peak - peak)
    weights = jnp.exp(scores - peak[:, :, None]).astype(jnp.bfloat16)
    weighted = joined[:, :, :LATENT_CHANNELS] * shrink[:, :, None] + jnp.einsum(
        "oep,opf->oef", weights, fresh[:, :, :LATENT_CHANNELS], preferred_element_type=jnp.float32
    )
    total = cache_total * shrink + jnp.sum(weights.astype(jnp.float32), axis=2)
    return (weighted / total[:, :, None]).astype(jnp.bfloat16)


def over_seq(x):
    return lax.all_to_all(x, "seq", split_axis=0, concat_axis=0, tiled=True)


def along(x, d):
    return lax.ppermute(x, "grp", [(i, (i + d) % 4) for i in range(4)])


def local(
    compressed,
    block_channel_scale,
    outlier_channels,
    outlier_values,
    lengths,
    assignment,
    padding,
    queries,
    decode_token_latent,
):
    group_here = lax.axis_index("grp")
    seq_here = lax.axis_index("seq")
    rows_here = [lax.dynamic_index_in_dim(x, group_here, 0, keepdims=False) for x in (lengths, assignment, padding)]
    table = jnp.concatenate([jnp.stack([group_here, seq_here]).astype(jnp.int32)] + rows_here)
    packed = compressed.T
    channels = outlier_channels.T

    starts = [sum(CHUNKS[:i]) for i in range(len(CHUNKS))]
    last = len(CHUNKS) - 1
    latent = [
        dequantize(start, rows, table, packed, block_channel_scale, channels, outlier_values)
        for start, rows in zip(starts, CHUNKS)
    ]
    turned = queries.transpose(0, 2, 1)
    pieces = [along(x, d) for d, x in zip((1, 2, 3), split(table, turned))]

    stripes, *pieces = lax.optimization_barrier((over_seq(latent[0]), *pieces))
    partial = attend(table, turned, pieces, latent)
    cache = None
    for i, start in enumerate(starts):
        (two,) = pack(table, stripes, (2,))
        if i < last:
            stripes, chunk, two = lax.optimization_barrier((stripes, latent[i + 1], two))
        else:
            stripes, two = lax.optimization_barrier((stripes, two))
        one, three = pack(table, stripes, (1, 3))
        two = along(two, 2)
        if i == 0:
            one, two, three, partial = lax.optimization_barrier((one, two, three, partial))
        else:
            one, two, three = lax.optimization_barrier((one, two, three))
        step = [along(one, 1), two, along(three, 3)]
        if i < last:
            cache = own(start, table, stripes, cache)
            cache = put(start, table, (2,), step[1:2], cache)
            stripes = over_seq(chunk)
            if i == last - 1:
                partial, cache = lax.optimization_barrier((partial, cache, stripes))[:2]
                partials = over_seq(partial.reshape(32, 16, -1))
                stripes, partials, *step = lax.optimization_barrier((stripes, partials, *step))
            else:
                stripes, cache, *step = lax.optimization_barrier((stripes, cache, *step))
            before = (start, step)

    joined = lax.all_to_all(join(table, partials), "grp", split_axis=0, concat_axis=0, tiled=True)
    cache = put(before[0], table, (1, 3), before[1][::2], cache)
    cache = own(start, table, stripes, cache)
    cache = put(start, table, (2,), step[1:2], cache)
    joined, cache = lax.optimization_barrier((joined, cache))
    cache = put(start, table, (1, 3), step[::2], cache)
    attended = finish(joined, queries, decode_token_latent, seq_here)
    return cache.transpose(0, 1, 3, 2)[None, :, None], attended


def solution(mesh):
    placed = (
        P(("grp", "seq"), None),
        P(("grp", "seq"), None),
        P(("grp", "seq"), None),
        P(("grp", "seq"), None, None),
        P(),
        P(),
        P(),
        P("grp", None, None),
        P("grp", None, None),
    )
    return jax.shard_map(
        local,
        mesh=mesh,
        in_specs=placed,
        out_specs=(P("grp", None, "seq", None, None, None), P("grp", "seq", None)),
        check_vma=False,
    )
```

```python
import functools

import jax
import jax.numpy as jnp
from jax import lax
from jax.experimental import pallas as pl
from jax.experimental.pallas import tpu as pltpu
from jax.sharding import PartitionSpec as P

LATENT_CHANNELS = 512
MOST_STRIPES = 12
HEADS = 128
NEG_FILL = -1e30
SCORE_SCALE = 192.0 ** (-0.5)
CHUNKS = (256, 320)
KEY_TILE = 16
KEY_PART = 4
NOTE_LANES = 128

SMEM = pl.BlockSpec(memory_space=pltpu.SMEM)
HBM = pl.BlockSpec(memory_space=pltpu.HBM)
VMEM = pl.BlockSpec(memory_space=pltpu.VMEM)


LONG = pl.CostEstimate(flops=40 << 30, bytes_accessed=0, transcendentals=0)


def params(megabytes=16):
    return pltpu.CompilerParams(vmem_limit_bytes=megabytes << 20)


def moved(steps, rows):
    size = 2 * steps * MOST_STRIPES * rows * 128
    return pl.CostEstimate(flops=0, bytes_accessed=2 * size, transcendentals=0)


def request_for(table, target):
    first, count, before = 0, 0, 0
    for r in range(4):
        here = table[2 + r]
        hit = table[6 + r] == target
        first = jnp.where(hit, before, first)
        count = jnp.where(hit, here, count)
        before = before + here
    return first, count


def request_of(table, stripe):
    target, empty, before = 0, 0, 0
    for r in range(4):
        after = before + table[2 + r]
        inside = jnp.logical_and(stripe >= before, stripe < after)
        target = jnp.where(inside, table[6 + r], target)
        empty = jnp.where(stripe == after - 1, table[10 + r], empty)
        before = after
    return target, empty


def dequantize_kernel(start, per_step, total, table, packed, scale, channels, values, out, scales, marks):
    rows = packed.shape[0]
    width = per_step * 16
    step = pl.program_id(0)

    @pl.when(step == 0)
    def _():
        mark = channels[...].astype(jnp.float32).T
        low, high = start // 128 * 128, min(-(-(start + rows) // 128) * 128, scale.shape[1])
        plain = scale[:, low:high]
        ids = (lax.broadcasted_iota(jnp.int32, plain.shape, 1) + low).astype(jnp.float32)
        for k in range(16):
            plain = jnp.where(ids == mark[:, k : k + 1], 0.0, plain)
        turned = plain.T[start - low : start - low + rows]
        for i in range(total):
            scales[i] = turned[:, i * per_step : (i + 1) * per_step]
            marks[i] = jnp.concatenate([mark[i * per_step + b : i * per_step + b + 1] for b in range(per_step)], axis=1)

    _, empty = request_of(table, table[1])
    ids = (lax.broadcasted_iota(jnp.int32, (rows, width), 0) + start).astype(jnp.float32)
    onehot = (ids == marks[step]).astype(jnp.bfloat16)
    flat = values[...].reshape(width, 128)
    block = lax.broadcasted_iota(jnp.int32, (width, 128), 0) // 16
    spread = jnp.concatenate([jnp.where(block == b, flat, jnp.zeros_like(flat)) for b in range(per_step)], axis=1)
    outliers = jnp.dot(onehot, spread, preferred_element_type=jnp.float32)
    tokens = lax.broadcasted_iota(jnp.int32, (rows, 128), 1)
    here = scales[step]
    for b in range(per_step):
        lanes = slice(b * 128, (b + 1) * 128)
        latent = packed[:, lanes].astype(jnp.float32) * here[:, b : b + 1] + outliers[:, lanes]
        if b == per_step - 1:
            limit = jnp.where(step == total - 1, 128 - empty, 128)
            latent = jnp.where(tokens < limit, latent, 0.0)
        out[b] = latent.astype(jnp.bfloat16)


def dequantize(start, rows, table, packed, scale, channels, values, cost):
    packed, values = [pltpu.with_memory_space_constraint(x, pltpu.HBM) for x in (packed, values)]
    blocks = scale.shape[0]
    per_step = 16
    steps = blocks // per_step
    return pl.pallas_call(
        functools.partial(dequantize_kernel, start, per_step, steps),
        grid=(steps,),
        out_shape=pltpu.HBM((blocks, rows, 128), jnp.bfloat16),
        in_specs=[
            SMEM,
            pl.BlockSpec((pl.Element(rows), pl.Element(per_step * 128)), lambda i: (start, i * per_step * 128)),
            pl.BlockSpec(scale.shape, lambda i: (0, 0)),
            pl.BlockSpec(channels.shape, lambda i: (0, 0)),
            pl.BlockSpec((per_step, 16, 128), lambda i: (i, 0, 0)),
        ],
        out_specs=pl.BlockSpec((per_step, rows, 128), lambda i: (i, 0, 0)),
        scratch_shapes=[
            pltpu.VMEM((steps, rows, per_step), jnp.float32),
            pltpu.VMEM((steps, 1, per_step * 16), jnp.float32),
        ],
        compiler_params=params(60),
        cost_estimate=pl.CostEstimate(flops=0, bytes_accessed=4 * blocks * rows * 128, transcendentals=0),
        name="dequantize",
    )(table, packed, scale, channels, values)


def collect(table, steps, stripes, targets, zeros, sems):
    zeros[...] = jnp.zeros_like(zeros)
    for i, d in enumerate(steps):
        first, count = request_for(table, lax.rem(table[0] + d, 4))
        for v in range(MOST_STRIPES):

            @pl.when(v < count)
            def _():
                pltpu.make_async_copy(stripes.at[first + v], targets[i].at[v], sems.at[i]).start()

            @pl.when(v >= count)
            def _():
                pltpu.make_async_copy(zeros, targets[i].at[v], sems.at[i]).start()

    for i in range(len(steps)):
        pltpu.make_async_copy(targets[i], targets[i], sems.at[i]).wait()


def collect_scratch(steps, rows):
    return [pltpu.VMEM((rows, 128), jnp.bfloat16), pltpu.SemaphoreType.DMA((steps,))]


def pack_kernel(steps, table, stripes, *refs):
    outs, scratch = refs[: len(steps)], refs[len(steps) :]
    collect(table, steps, stripes, outs, *scratch)


def pack(table, stripes, steps):
    rows = stripes.shape[1]
    one = pltpu.HBM((MOST_STRIPES, rows, 128), jnp.bfloat16)
    return pl.pallas_call(
        functools.partial(pack_kernel, steps),
        out_shape=(one,) * len(steps),
        in_specs=[SMEM, VMEM],
        out_specs=(HBM,) * len(steps),
        scratch_shapes=collect_scratch(len(steps), rows),
        compiler_params=params(),
        cost_estimate=moved(len(steps), rows),
        name="pack",
    )(table, stripes)


def own_kernel(start, table, stripes, *refs):
    out, scratch = refs[-3], refs[-2:]
    rows = stripes.shape[1]
    collect(table, (0,), stripes, [out.at[table[0], :, pl.ds(start, rows), :]], *scratch)


def own(start, table, stripes, cache, cost=None):
    rows = stripes.shape[1]
    more = () if cache is None else (cache,)
    return pl.pallas_call(
        functools.partial(own_kernel, start),
        out_shape=jax.ShapeDtypeStruct((4, MOST_STRIPES, sum(CHUNKS), 128), jnp.bfloat16),
        in_specs=[SMEM, VMEM] + [HBM] * len(more),
        out_specs=HBM,
        input_output_aliases={2: 0} if more else {},
        scratch_shapes=collect_scratch(1, rows),
        compiler_params=params(),
        cost_estimate=cost or moved(1, rows),
        name="own",
    )(table, stripes, *more)


PIECES = 3


def put_copies(start, steps, table, arrived, out, sems):
    rows, size = arrived[0].shape[1], MOST_STRIPES // PIECES
    copies = []
    for i, d in enumerate(steps):
        slot = out.at[lax.rem(table[0] + 4 - d, 4)]
        for h in range(PIECES):
            part = pl.ds(h * size, size)
            copies.append(
                pltpu.make_async_copy(arrived[i].at[part], slot.at[part, pl.ds(start, rows), :], sems.at[i, h])
            )
    return copies


def put_kernel(start, steps, table, *refs):
    arrived, (out, sems) = refs[: len(steps)], refs[-2:]
    copies = put_copies(start, steps, table, arrived, out, sems)
    for copy in copies:
        copy.start()
    for copy in copies:
        copy.wait()


def put_later_kernel(start, steps, table, *refs):
    arrived, (out, sems, held, in_sems) = refs[: len(steps)], refs[-4:]
    come = [pltpu.make_async_copy(arrived[i], held.at[i], in_sems.at[i]) for i in range(len(steps))]
    leave = put_copies(start, steps, table, [held.at[i] for i in range(len(steps))], out, sems)
    for copy in come:
        copy.start()
    for i, copy in enumerate(come):
        copy.wait()
        for part in leave[i * PIECES : (i + 1) * PIECES]:
            part.start()
    for part in leave:
        part.wait()


def put(start, table, steps, arrived, cache, later=False):
    rows = arrived[0].shape[1]
    scratch = [pltpu.SemaphoreType.DMA((len(steps), PIECES))]
    if later:
        scratch += [
            pltpu.VMEM((len(steps), MOST_STRIPES, rows, 128), jnp.bfloat16),
            pltpu.SemaphoreType.DMA((len(steps),)),
        ]
    return pl.pallas_call(
        functools.partial(put_later_kernel if later else put_kernel, start, steps),
        out_shape=jax.ShapeDtypeStruct((4, MOST_STRIPES, sum(CHUNKS), 128), jnp.bfloat16),
        in_specs=[SMEM] + [pl.BlockSpec(memory_space=pl.ANY) if later else VMEM] * len(steps) + [HBM],
        out_specs=HBM,
        input_output_aliases={len(steps) + 1: 0},
        scratch_shapes=scratch,
        compiler_params=params(),
        cost_estimate=moved(len(steps), rows),
        name="put",
    )(table, *arrived, cache)


def partner(table):
    return table[1] + 1 - 2 * lax.rem(table[1], 2)


def half_of(table, rows):
    return pl.ds(pl.multiple_of(lax.rem(table[1], 2) * rows, rows), rows)


def split_kernel(table, queries, *refs):
    outs, (held, in_sems, out_sems) = refs[:3], refs[3:]
    half = half_of(table, held.shape[1])
    come = [
        pltpu.make_async_copy(queries.at[lax.rem(table[0] + d + 1, 4), half], held.at[d], in_sems.at[d])
        for d in range(3)
    ]
    leave = [pltpu.make_async_copy(held.at[d], outs[d], out_sems.at[d]) for d in range(3)]
    for copy in come:
        copy.start()
    for d in range(3):
        come[d].wait()
        leave[d].start()
    for copy in leave:
        copy.wait()


def split(table, queries):
    shape = (queries.shape[1] // 2, queries.shape[2])
    return pl.pallas_call(
        split_kernel,
        out_shape=(pltpu.HBM(shape, queries.dtype),) * 3,
        in_specs=[SMEM, HBM],
        out_specs=(HBM,) * 3,
        scratch_shapes=[
            pltpu.VMEM((3,) + shape, queries.dtype),
            pltpu.SemaphoreType.DMA((3,)),
            pltpu.SemaphoreType.DMA((3,)),
        ],
        compiler_params=params(),
        cost_estimate=pl.CostEstimate(flops=0, bytes_accessed=1 << 20, transcendentals=0),
        name="split",
    )(table, pltpu.with_memory_space_constraint(queries, pltpu.HBM))


def start_half(table, target, queries, pieces, out, sem):
    for d in range(4):
        source = queries.at[table[0], half_of(table, out.shape[0])] if d == 0 else pieces[d - 1]

        @pl.when(target == lax.rem(table[0] + 4 - d, 4))
        def _():
            pltpu.make_async_copy(source, out, sem).start()


def hand_kernel(table, queries, in1, in2, in3, out, sem):
    target, _ = request_of(table, partner(table))
    start_half(table, target, queries, (in1, in2, in3), out, sem)
    pltpu.make_async_copy(in1, out, sem).wait()


def hand(table, queries, pieces):
    queries = pltpu.with_memory_space_constraint(queries, pltpu.HBM)
    return pl.pallas_call(
        hand_kernel,
        out_shape=jax.ShapeDtypeStruct(pieces[0].shape, pieces[0].dtype),
        in_specs=[SMEM, HBM] + [VMEM] * 3,
        out_specs=VMEM,
        scratch_shapes=[pltpu.SemaphoreType.DMA],
        compiler_params=params(),
        cost_estimate=pl.CostEstimate(flops=0, bytes_accessed=1 << 20, transcendentals=0),
        name="hand",
    )(table, queries, *pieces)


def in_three(x):
    high = x.astype(jnp.bfloat16)
    rest = x - high.astype(jnp.float32)
    middle = rest.astype(jnp.bfloat16)
    low = (rest - middle.astype(jnp.float32)).astype(jnp.bfloat16)
    return high, middle, low


def attend_kernel(steps, table, *refs):
    sources, handed, keys = refs[:4], refs[4], refs[5 : 5 + len(CHUNKS)]
    out, peak, total, weighted, turned, queries, sems = refs[5 + len(CHUNKS) :]
    step = pl.program_id(0)
    target, empty = request_of(table, table[1])

    @pl.when(step == 0)
    def _():
        rows = handed.shape[0]
        mine, other = turned.at[half_of(table, rows)], turned.at[half_of((0, partner(table)), rows)]
        start_half(table, target, sources[0], sources[1:], mine, sems.at[0])
        copy = pltpu.make_async_copy(handed, other, sems.at[1])
        copy.start()
        copy.wait()
        pltpu.make_async_copy(sources[1], mine, sems.at[0]).wait()
        queries[...] = turned[...].T
        peak[...] = jnp.full_like(peak, NEG_FILL)
        total[...] = jnp.zeros_like(total)
        weighted[...] = jnp.zeros_like(weighted)

    parts = [
        jnp.concatenate(
            [jnp.concatenate([k[b] for k in keys], axis=0) for b in range(i, i + KEY_PART)], axis=1
        )
        for i in range(0, KEY_TILE, KEY_PART)
    ]
    scores = [jnp.dot(queries[...], part, preferred_element_type=jnp.float32) for part in parts]
    limit = jnp.where(step == steps - 1, KEY_PART * 128 - empty, KEY_PART * 128)
    columns = lax.broadcasted_iota(jnp.int32, (1, KEY_PART * 128), 1)
    scores[-1] = scores[-1] + jnp.where(columns < limit, 0.0, NEG_FILL)
    before = peak[...]
    now = before
    for score in scores:
        now = jnp.maximum(now, jnp.max(score, axis=1, keepdims=True))
    shrink = jnp.exp((before - now) * SCORE_SCALE)
    whole, sums = total[...] * shrink, weighted[...] * shrink[:, :1]
    for score, part in zip(scores, parts):
        weights = jnp.exp((score - now[:, :1]) * SCORE_SCALE).astype(jnp.bfloat16)
        whole = whole + jnp.sum(weights.astype(jnp.float32), axis=1, keepdims=True)
        sums = sums + lax.dot_general(
            weights, part[:LATENT_CHANNELS], (((1,), (1,)), ((), ())), preferred_element_type=jnp.float32
        )
    total[...], weighted[...], peak[...] = whole, sums, now

    @pl.when(step == steps - 1)
    def _():
        out[:, :LATENT_CHANNELS] = weighted[...].astype(jnp.bfloat16)
        lane = lax.broadcasted_iota(jnp.int32, peak.shape, 1)
        note = jnp.zeros(peak.shape, jnp.float32)
        for i, part in enumerate(in_three(peak[...] * SCORE_SCALE) + in_three(total[...])):
            note = jnp.where(lane == i, part.astype(jnp.float32), note)
        out[:, LATENT_CHANNELS:] = note.astype(jnp.bfloat16)


def attend(table, queries, pieces, handed, keys):
    channels, rows = queries.shape[1:]
    queries = pltpu.with_memory_space_constraint(queries, pltpu.HBM)
    keys = [pltpu.with_memory_space_constraint(k, pltpu.HBM) for k in keys]
    blocks = keys[0].shape[0]
    steps = blocks // KEY_TILE
    width = LATENT_CHANNELS + NOTE_LANES
    return pl.pallas_call(
        functools.partial(attend_kernel, steps),
        grid=(steps,),
        out_shape=jax.ShapeDtypeStruct((rows, width), jnp.bfloat16),
        in_specs=[SMEM, HBM] + [VMEM] * 4
        + [pl.BlockSpec((KEY_TILE,) + k.shape[1:], lambda i: (i, 0, 0)) for k in keys],
        out_specs=pl.BlockSpec((rows, width), lambda i: (0, 0)),
        scratch_shapes=[
            pltpu.VMEM((rows, 128), jnp.float32),
            pltpu.VMEM((rows, 128), jnp.float32),
            pltpu.VMEM((rows, LATENT_CHANNELS), jnp.float32),
            pltpu.VMEM((channels, rows), jnp.bfloat16),
            pltpu.VMEM((rows, channels), jnp.bfloat16),
            pltpu.SemaphoreType.DMA((2,)),
        ],
        compiler_params=params(60),
        cost_estimate=LONG,
        name="attend",
    )(table, queries, *pieces, handed, *keys)


def join_kernel(table, partials, out):
    stripes, rows, _ = partials.shape
    note = partials[:, :, LATENT_CHANNELS:].astype(jnp.float32)
    peak = note[:, :, 0:1] + note[:, :, 1:2] + note[:, :, 2:3]
    total = note[:, :, 3:4] + note[:, :, 4:5] + note[:, :, 5:6]
    stripe = lax.broadcasted_iota(jnp.int32, peak.shape, 0)
    lane = lax.broadcasted_iota(jnp.int32, (rows, NOTE_LANES), 1)
    values = partials[:, :, :LATENT_CHANNELS].astype(jnp.float32)
    for d in range(4):
        first, count = request_for(table, d)
        inside = jnp.logical_and(stripe >= first, stripe < first + count)
        top = jnp.max(jnp.where(inside, peak, NEG_FILL), axis=0)
        factor = jnp.where(inside, jnp.exp(jnp.where(inside, peak, NEG_FILL) - top[None]), 0.0)
        out[d, :, :LATENT_CHANNELS] = jnp.sum(values * factor, axis=0)
        whole = jnp.sum(total * factor, axis=0)
        out[d, :, LATENT_CHANNELS:] = jnp.where(lane == 0, top, jnp.where(lane == 1, whole, 0.0))


def join(table, partials):
    return pl.pallas_call(
        join_kernel,
        out_shape=jax.ShapeDtypeStruct((4,) + partials.shape[1:], jnp.float32),
        in_specs=[SMEM, VMEM],
        out_specs=VMEM,
        compiler_params=params(),
        cost_estimate=pl.CostEstimate(flops=0, bytes_accessed=1 << 20, transcendentals=0),
        name="join",
    )(table, partials)


def finish_kernel(scores, fresh, joined, out):
    for slot in range(4):
        cache_peak = joined[slot, :, LATENT_CHANNELS : LATENT_CHANNELS + 1]
        cache_total = joined[slot, :, LATENT_CHANNELS + 1 : LATENT_CHANNELS + 2]
        peak = jnp.maximum(cache_peak, jnp.max(scores[slot], axis=1, keepdims=True))
        shrink = jnp.exp(cache_peak - peak)
        weights = jnp.exp(scores[slot] - peak).astype(jnp.bfloat16)
        weighted = joined[slot, :, :LATENT_CHANNELS] * shrink + jnp.dot(
            weights, fresh[slot][:, :LATENT_CHANNELS], preferred_element_type=jnp.float32
        )
        total = cache_total * shrink + jnp.sum(weights.astype(jnp.float32), axis=1, keepdims=True)
        out[slot] = (weighted / total).astype(jnp.bfloat16)


def finish(joined, queries, fresh, seq_here):
    own = joined.shape[1]
    row_start = seq_here * own
    own_queries = lax.dynamic_slice_in_dim(queries, row_start, own, 1)
    scores = (
        jnp.einsum("yeu,ynu->yen", own_queries, fresh, preferred_element_type=jnp.float32) * SCORE_SCALE
    )
    row_step = (row_start + jnp.arange(own, dtype=jnp.int32)) // HEADS
    col_step = jnp.arange(fresh.shape[1], dtype=jnp.int32)
    scores = jnp.where((col_step[None, :] <= row_step[:, None])[None], scores, NEG_FILL)
    return pl.pallas_call(
        finish_kernel,
        out_shape=jax.ShapeDtypeStruct((4, own, LATENT_CHANNELS), jnp.bfloat16),
        in_specs=[VMEM] * 3,
        out_specs=VMEM,
        compiler_params=params(),
        cost_estimate=pl.CostEstimate(flops=0, bytes_accessed=1 << 20, transcendentals=0),
        name="finish",
    )(scores, fresh, joined)


def tie(*xs):
    return lax.optimization_barrier(xs)


def over_seq(x):
    return lax.all_to_all(x, "seq", split_axis=0, concat_axis=0, tiled=True)


def all_along(x):
    return lax.all_to_all(x, "grp", split_axis=0, concat_axis=0, tiled=True)


def along(x, d):
    return lax.ppermute(x, "grp", [(i, (i + d) % 4) for i in range(4)])


def local(
    compressed,
    block_channel_scale,
    outlier_channels,
    outlier_values,
    lengths,
    assignment,
    padding,
    queries,
    decode_token_latent,
):
    group_here = lax.axis_index("grp")
    seq_here = lax.axis_index("seq")
    rows_here = [lax.dynamic_index_in_dim(x, group_here, 0, keepdims=False) for x in (lengths, assignment, padding)]
    table = jnp.concatenate([jnp.stack([group_here, seq_here]).astype(jnp.int32)] + rows_here)
    packed = compressed.T
    channels = outlier_channels.T

    starts = [sum(CHUNKS[:i]) for i in range(len(CHUNKS))]
    last = len(CHUNKS) - 1
    latent = [
        dequantize(
            start, rows, table, packed, block_channel_scale, channels, outlier_values, LONG if start == starts[-1] else None
        )
        for start, rows in zip(starts, CHUNKS)
    ]
    turned = queries.transpose(0, 2, 1)
    latent[0], turned = tie(latent[0], turned)
    pieces = [along(x, d) for d, x in zip((1, 2, 3), split(table, turned))]
    handed = hand(table, turned, pieces)

    stripes, latent[1], handed, *pieces = tie(over_seq(latent[0]), latent[1], handed, *pieces)

    one, two, three = pack(table, stripes, (1, 2, 3))
    stripes, following, one, two, three = tie(stripes, latent[1], one, two, three)
    two = along(two, 2)
    handed = lax.ppermute(handed, "seq", [(j, j ^ 1) for j in range(32)])
    partial = attend(table, turned, pieces, handed, latent)
    one, two, three, partial = tie(one, two, three, partial)
    first = [along(one, 1), along(three, 3)]
    cache = put(starts[0], table, (2,), (two,), own(starts[0], table, stripes, None))
    stripes, cache, partial, *first = tie(over_seq(following), cache, partial, *first)

    one, two, three = pack(table, stripes, (1, 2, 3))
    stripes, cache, one, two, three = tie(stripes, cache, one, two, three)
    cache = own(starts[1], table, stripes, cache, LONG)
    following, cache = tie(partial.reshape(32, 16, -1), cache)
    second = [along(one, 1), along(three, 3)]
    two = along(two, 2)
    joined = all_along(join(table, over_seq(following)))
    cache = put(starts[0], table, (1, 3), first, cache, later=True)
    cache = put(starts[1], table, (2,), (two,), cache)
    joined, cache = tie(joined, cache)
    attended = finish(joined, queries, decode_token_latent, seq_here)
    attended, cache = tie(attended, cache)
    cache = put(starts[1], table, (1, 3), second, cache)
    return cache.transpose(0, 1, 3, 2)[None, :, None], attended


def solution(mesh):
    placed = (
        P(("grp", "seq"), None),
        P(("grp", "seq"), None),
        P(("grp", "seq"), None),
        P(("grp", "seq"), None, None),
        P(),
        P(),
        P(),
        P("grp", None, None),
        P("grp", None, None),
    )
    return jax.shard_map(
        local,
        mesh=mesh,
        in_specs=placed,
        out_specs=(P("grp", None, "seq", None, None, None), P("grp", "seq", None)),
        check_vma=False,
    )
```

```python
import functools

import jax
import jax.numpy as jnp
from jax import lax
from jax.experimental import pallas as pl
from jax.experimental.pallas import tpu as pltpu
from jax.sharding import PartitionSpec as P

LATENT_CHANNELS = 512
MOST_STRIPES = 12
HEADS = 128
NEG_FILL = -1e30
SCORE_SCALE = 192.0 ** (-0.5)
CHUNKS = (272, 304)
KEY_TILE = 16
KEY_PART = 4
NOTE_LANES = 128

SMEM = pl.BlockSpec(memory_space=pltpu.SMEM)
HBM = pl.BlockSpec(memory_space=pltpu.HBM)
VMEM = pl.BlockSpec(memory_space=pltpu.VMEM)


LONG = pl.CostEstimate(flops=40 << 30, bytes_accessed=0, transcendentals=0)


def params(megabytes=16):
    return pltpu.CompilerParams(vmem_limit_bytes=megabytes << 20)


def moved(steps, rows):
    size = 2 * steps * MOST_STRIPES * rows * 128
    return pl.CostEstimate(flops=0, bytes_accessed=2 * size, transcendentals=0)


def request_for(table, target):
    first, count, before = 0, 0, 0
    for r in range(4):
        here = table[2 + r]
        hit = table[6 + r] == target
        first = jnp.where(hit, before, first)
        count = jnp.where(hit, here, count)
        before = before + here
    return first, count


def request_of(table, stripe):
    target, empty, before = 0, 0, 0
    for r in range(4):
        after = before + table[2 + r]
        inside = jnp.logical_and(stripe >= before, stripe < after)
        target = jnp.where(inside, table[6 + r], target)
        empty = jnp.where(stripe == after - 1, table[10 + r], empty)
        before = after
    return target, empty


def dequantize_kernel(start, per_step, total, place, lengths, padding, packed, scale, channels, values, out, scales, marks):
    rows = packed.shape[0]
    width = per_step * 16
    step = pl.program_id(0)

    @pl.when(step == 0)
    def _():
        mark = channels[...].astype(jnp.float32).T
        low, high = start // 128 * 128, min(-(-(start + rows) // 128) * 128, scale.shape[1])
        plain = scale[:, low:high]
        ids = (lax.broadcasted_iota(jnp.int32, plain.shape, 1) + low).astype(jnp.float32)
        for k in range(16):
            plain = jnp.where(ids == mark[:, k : k + 1], 0.0, plain)
        turned = plain.T[start - low : start - low + rows]
        for i in range(total):
            scales[i] = turned[:, i * per_step : (i + 1) * per_step]
            marks[i] = jnp.concatenate([mark[i * per_step + b : i * per_step + b + 1] for b in range(per_step)], axis=1)

    group, empty, before = place[0], 0, 0
    for r in range(4):
        before = before + lengths[group, r]
        empty = jnp.where(place[1] == before - 1, padding[group, r], empty)
    ids = (lax.broadcasted_iota(jnp.int32, (rows, width), 0) + start).astype(jnp.float32)
    onehot = (ids == marks[step]).astype(jnp.bfloat16)
    flat = values[...].reshape(width, 128)
    block = lax.broadcasted_iota(jnp.int32, (width, 128), 0) // 16
    spread = jnp.concatenate([jnp.where(block == b, flat, jnp.zeros_like(flat)) for b in range(per_step)], axis=1)
    outliers = jnp.dot(onehot, spread, preferred_element_type=jnp.float32)
    tokens = lax.broadcasted_iota(jnp.int32, (rows, 128), 1)
    here = scales[step]
    for b in range(per_step):
        lanes = slice(b * 128, (b + 1) * 128)
        latent = packed[:, lanes].astype(jnp.float32) * here[:, b : b + 1] + outliers[:, lanes]
        if b == per_step - 1:
            limit = jnp.where(step == total - 1, 128 - empty, 128)
            latent = jnp.where(tokens < limit, latent, 0.0)
        out[b] = latent.astype(jnp.bfloat16)


def dequantize(start, rows, place, lengths, padding, packed, scale, channels, values):
    packed, values = [pltpu.with_memory_space_constraint(x, pltpu.HBM) for x in (packed, values)]
    blocks = scale.shape[0]
    per_step = 16
    steps = blocks // per_step
    return pl.pallas_call(
        functools.partial(dequantize_kernel, start, per_step, steps),
        grid=(steps,),
        out_shape=pltpu.HBM((blocks, rows, 128), jnp.bfloat16),
        in_specs=[
            SMEM,
            SMEM,
            SMEM,
            pl.BlockSpec((pl.Element(rows), pl.Element(per_step * 128)), lambda i: (start, i * per_step * 128)),
            pl.BlockSpec(scale.shape, lambda i: (0, 0)),
            pl.BlockSpec(channels.shape, lambda i: (0, 0)),
            pl.BlockSpec((per_step, 16, 128), lambda i: (i, 0, 0)),
        ],
        out_specs=pl.BlockSpec((per_step, rows, 128), lambda i: (i, 0, 0)),
        scratch_shapes=[
            pltpu.VMEM((steps, rows, per_step), jnp.float32),
            pltpu.VMEM((steps, 1, per_step * 16), jnp.float32),
        ],
        compiler_params=params(60),
        cost_estimate=pl.CostEstimate(flops=0, bytes_accessed=4 * blocks * rows * 128, transcendentals=0),
        name="dequantize",
    )(place, lengths, padding, packed, scale, channels, values)


def collect(table, d, stripes, target, zeros, sem):
    first, count = request_for(table, lax.rem(table[0] + d, 4))
    for v in range(MOST_STRIPES):

        @pl.when(v < count)
        def _():
            pltpu.make_async_copy(stripes.at[first + v], target.at[v], sem).start()

        @pl.when(v >= count)
        def _():
            pltpu.make_async_copy(zeros, target.at[v], sem).start()


def pack_kernel(start, table, stripes, *refs):
    *outs, cache, zeros, sems = refs[-6:]
    zeros[...] = jnp.zeros_like(zeros)
    targets = [cache.at[table[0], :, pl.ds(start, stripes.shape[1]), :], *outs]
    for d in (2, 1, 3, 0):
        collect(table, d, stripes, targets[d], zeros, sems.at[d])
    for d, target in enumerate(targets):
        pltpu.make_async_copy(target, target, sems.at[d]).wait()


def pack(start, table, stripes, cache):
    rows = stripes.shape[1]
    more = () if cache is None else (cache,)
    one = pltpu.HBM((MOST_STRIPES, rows, 128), jnp.bfloat16)
    return pl.pallas_call(
        functools.partial(pack_kernel, start),
        out_shape=(one, one, one, jax.ShapeDtypeStruct((4, MOST_STRIPES, sum(CHUNKS), 128), jnp.bfloat16)),
        in_specs=[SMEM, VMEM] + [HBM] * len(more),
        out_specs=(HBM,) * 4,
        input_output_aliases={2: 3} if more else {},
        scratch_shapes=[pltpu.VMEM((rows, 128), jnp.bfloat16), pltpu.SemaphoreType.DMA((4,))],
        compiler_params=params(),
        cost_estimate=moved(4, rows),
        name="pack",
    )(table, stripes, *more)


PIECES = 3


def put_copies(start, steps, table, arrived, out, sems):
    rows, size = arrived[0].shape[1], MOST_STRIPES // PIECES
    copies = []
    for i, d in enumerate(steps):
        slot = out.at[lax.rem(table[0] + 4 - d, 4)]
        for h in range(PIECES):
            part = pl.ds(h * size, size)
            copies.append(
                pltpu.make_async_copy(arrived[i].at[part], slot.at[part, pl.ds(start, rows), :], sems.at[i, h])
            )
    return copies


def put_kernel(start, steps, table, *refs):
    arrived, (out, sems) = refs[: len(steps)], refs[-2:]
    copies = put_copies(start, steps, table, arrived, out, sems)
    for copy in copies:
        copy.start()
    for copy in copies:
        copy.wait()


def put_later_kernel(start, steps, table, *refs):
    arrived, (out, sems, held, in_sems) = refs[: len(steps)], refs[-4:]
    come = [pltpu.make_async_copy(arrived[i], held.at[i], in_sems.at[i]) for i in range(len(steps))]
    leave = put_copies(start, steps, table, [held.at[i] for i in range(len(steps))], out, sems)
    for copy in come:
        copy.start()
    for i, copy in enumerate(come):
        copy.wait()
        for part in leave[i * PIECES : (i + 1) * PIECES]:
            part.start()
    for part in leave:
        part.wait()


def put(start, table, steps, arrived, cache, later=False, cost=None):
    rows = arrived[0].shape[1]
    scratch = [pltpu.SemaphoreType.DMA((len(steps), PIECES))]
    if later:
        scratch += [
            pltpu.VMEM((len(steps), MOST_STRIPES, rows, 128), jnp.bfloat16),
            pltpu.SemaphoreType.DMA((len(steps),)),
        ]
    return pl.pallas_call(
        functools.partial(put_later_kernel if later else put_kernel, start, steps),
        out_shape=jax.ShapeDtypeStruct((4, MOST_STRIPES, sum(CHUNKS), 128), jnp.bfloat16),
        in_specs=[SMEM] + [pl.BlockSpec(memory_space=pl.ANY) if later else VMEM] * len(steps) + [HBM],
        out_specs=HBM,
        input_output_aliases={len(steps) + 1: 0},
        scratch_shapes=scratch,
        compiler_params=params(),
        cost_estimate=cost or moved(len(steps), rows),
        name="put",
    )(table, *arrived, cache)


def partner(table):
    return table[1] + 1 - 2 * lax.rem(table[1], 2)


def half_of(table, rows):
    return pl.ds(pl.multiple_of(lax.rem(table[1], 2) * rows, rows), rows)


def split_kernel(table, queries, *refs):
    outs, (held, in_sems, out_sems) = refs[:3], refs[3:]
    half = half_of(table, held.shape[1])
    come = [
        pltpu.make_async_copy(queries.at[lax.rem(table[0] + d + 1, 4), half], held.at[d], in_sems.at[d])
        for d in range(3)
    ]
    leave = [pltpu.make_async_copy(held.at[d], outs[d], out_sems.at[d]) for d in range(3)]
    for copy in come:
        copy.start()
    for d in range(3):
        come[d].wait()
        leave[d].start()
    for copy in leave:
        copy.wait()


def split(table, queries):
    shape = (queries.shape[1] // 2, queries.shape[2])
    return pl.pallas_call(
        split_kernel,
        out_shape=(pltpu.HBM(shape, queries.dtype),) * 3,
        in_specs=[SMEM, HBM],
        out_specs=(HBM,) * 3,
        scratch_shapes=[
            pltpu.VMEM((3,) + shape, queries.dtype),
            pltpu.SemaphoreType.DMA((3,)),
            pltpu.SemaphoreType.DMA((3,)),
        ],
        compiler_params=params(),
        cost_estimate=pl.CostEstimate(flops=0, bytes_accessed=1 << 20, transcendentals=0),
        name="split",
    )(table, pltpu.with_memory_space_constraint(queries, pltpu.HBM))


def start_half(table, target, queries, pieces, out, sem):
    for d in range(4):
        source = queries.at[table[0], half_of(table, out.shape[0])] if d == 0 else pieces[d - 1]

        @pl.when(target == lax.rem(table[0] + 4 - d, 4))
        def _():
            pltpu.make_async_copy(source, out, sem).start()


def hand_kernel(table, queries, in1, in2, in3, out, sem):
    target, _ = request_of(table, partner(table))
    start_half(table, target, queries, (in1, in2, in3), out, sem)
    pltpu.make_async_copy(in1, out, sem).wait()


def hand(table, queries, pieces):
    queries = pltpu.with_memory_space_constraint(queries, pltpu.HBM)
    return pl.pallas_call(
        hand_kernel,
        out_shape=jax.ShapeDtypeStruct(pieces[0].shape, pieces[0].dtype),
        in_specs=[SMEM, HBM] + [VMEM] * 3,
        out_specs=VMEM,
        scratch_shapes=[pltpu.SemaphoreType.DMA],
        compiler_params=params(),
        cost_estimate=pl.CostEstimate(flops=0, bytes_accessed=1 << 20, transcendentals=0),
        name="hand",
    )(table, queries, *pieces)


def in_three(x):
    high = x.astype(jnp.bfloat16)
    rest = x - high.astype(jnp.float32)
    middle = rest.astype(jnp.bfloat16)
    low = (rest - middle.astype(jnp.float32)).astype(jnp.bfloat16)
    return high, middle, low


def attend_kernel(steps, table, *refs):
    sources, handed, keys = refs[:4], refs[4], refs[5 : 5 + len(CHUNKS)]
    out, peak, total, weighted, turned, queries, sems = refs[5 + len(CHUNKS) :]
    step = pl.program_id(0)
    target, empty = request_of(table, table[1])

    @pl.when(step == 0)
    def _():
        rows = handed.shape[0]
        mine, other = turned.at[half_of(table, rows)], turned.at[half_of((0, partner(table)), rows)]
        start_half(table, target, sources[0], sources[1:], mine, sems.at[0])
        copy = pltpu.make_async_copy(handed, other, sems.at[1])
        copy.start()
        copy.wait()
        pltpu.make_async_copy(sources[1], mine, sems.at[0]).wait()
        queries[...] = turned[...].T
        peak[...] = jnp.full_like(peak, NEG_FILL)
        total[...] = jnp.zeros_like(total)
        weighted[...] = jnp.zeros_like(weighted)

    parts = [
        jnp.concatenate(
            [jnp.concatenate([k[b] for k in keys], axis=0) for b in range(i, i + KEY_PART)], axis=1
        )
        for i in range(0, KEY_TILE, KEY_PART)
    ]
    scores = [jnp.dot(queries[...], part, preferred_element_type=jnp.float32) for part in parts]
    limit = jnp.where(step == steps - 1, KEY_PART * 128 - empty, KEY_PART * 128)
    columns = lax.broadcasted_iota(jnp.int32, (1, KEY_PART * 128), 1)
    scores[-1] = scores[-1] + jnp.where(columns < limit, 0.0, NEG_FILL)
    before = peak[...]
    now = before
    for score in scores:
        now = jnp.maximum(now, jnp.max(score, axis=1, keepdims=True))
    shrink = jnp.exp((before - now) * SCORE_SCALE)
    whole, sums = total[...] * shrink, weighted[...] * shrink[:, :1]
    for score, part in zip(scores, parts):
        weights = jnp.exp((score - now[:, :1]) * SCORE_SCALE).astype(jnp.bfloat16)
        whole = whole + jnp.sum(weights.astype(jnp.float32), axis=1, keepdims=True)
        sums = sums + lax.dot_general(
            weights, part[:LATENT_CHANNELS], (((1,), (1,)), ((), ())), preferred_element_type=jnp.float32
        )
    total[...], weighted[...], peak[...] = whole, sums, now

    @pl.when(step == steps - 1)
    def _():
        out[:, :LATENT_CHANNELS] = weighted[...].astype(jnp.bfloat16)
        lane = lax.broadcasted_iota(jnp.int32, peak.shape, 1)
        note = jnp.zeros(peak.shape, jnp.float32)
        for i, part in enumerate(in_three(peak[...] * SCORE_SCALE) + in_three(total[...])):
            note = jnp.where(lane == i, part.astype(jnp.float32), note)
        out[:, LATENT_CHANNELS:] = note.astype(jnp.bfloat16)


def attend(table, queries, pieces, handed, keys):
    channels, rows = queries.shape[1:]
    queries = pltpu.with_memory_space_constraint(queries, pltpu.HBM)
    keys = [pltpu.with_memory_space_constraint(k, pltpu.HBM) for k in keys]
    blocks = keys[0].shape[0]
    steps = blocks // KEY_TILE
    width = LATENT_CHANNELS + NOTE_LANES
    return pl.pallas_call(
        functools.partial(attend_kernel, steps),
        grid=(steps,),
        out_shape=pltpu.HBM((rows, width), jnp.bfloat16),
        in_specs=[SMEM, HBM] + [VMEM] * 4
        + [pl.BlockSpec((KEY_TILE,) + k.shape[1:], lambda i: (i, 0, 0)) for k in keys],
        out_specs=pl.BlockSpec((rows, width), lambda i: (0, 0)),
        scratch_shapes=[
            pltpu.VMEM((rows, 128), jnp.float32),
            pltpu.VMEM((rows, 128), jnp.float32),
            pltpu.VMEM((rows, LATENT_CHANNELS), jnp.float32),
            pltpu.VMEM((channels, rows), jnp.bfloat16),
            pltpu.VMEM((rows, channels), jnp.bfloat16),
            pltpu.SemaphoreType.DMA((2,)),
        ],
        compiler_params=params(44),
        cost_estimate=LONG,
        name="attend",
    )(table, queries, *pieces, handed, *keys)


def join_kernel(table, partials, out):
    stripes, rows, _ = partials.shape
    note = partials[:, :, LATENT_CHANNELS:].astype(jnp.float32)
    peak = note[:, :, 0:1] + note[:, :, 1:2] + note[:, :, 2:3]
    total = note[:, :, 3:4] + note[:, :, 4:5] + note[:, :, 5:6]
    stripe = lax.broadcasted_iota(jnp.int32, peak.shape, 0)
    lane = lax.broadcasted_iota(jnp.int32, (rows, NOTE_LANES), 1)
    values = partials[:, :, :LATENT_CHANNELS].astype(jnp.float32)
    for d in range(4):
        first, count = request_for(table, d)
        inside = jnp.logical_and(stripe >= first, stripe < first + count)
        top = jnp.max(jnp.where(inside, peak, NEG_FILL), axis=0)
        factor = jnp.where(inside, jnp.exp(jnp.where(inside, peak, NEG_FILL) - top[None]), 0.0)
        out[d, :, :LATENT_CHANNELS] = jnp.sum(values * factor, axis=0)
        whole = jnp.sum(total * factor, axis=0)
        out[d, :, LATENT_CHANNELS:] = jnp.where(lane == 0, top, jnp.where(lane == 1, whole, 0.0))


def join(table, partials):
    return pl.pallas_call(
        join_kernel,
        out_shape=jax.ShapeDtypeStruct((4,) + partials.shape[1:], jnp.float32),
        in_specs=[SMEM, VMEM],
        out_specs=VMEM,
        compiler_params=params(),
        cost_estimate=pl.CostEstimate(flops=0, bytes_accessed=1 << 20, transcendentals=0),
        name="join",
    )(table, partials)


def finish_kernel(scores, fresh, joined, out):
    for slot in range(4):
        cache_peak = joined[slot, :, LATENT_CHANNELS : LATENT_CHANNELS + 1]
        cache_total = joined[slot, :, LATENT_CHANNELS + 1 : LATENT_CHANNELS + 2]
        peak = jnp.maximum(cache_peak, jnp.max(scores[slot], axis=1, keepdims=True))
        shrink = jnp.exp(cache_peak - peak)
        weights = jnp.exp(scores[slot] - peak).astype(jnp.bfloat16)
        weighted = joined[slot, :, :LATENT_CHANNELS] * shrink + jnp.dot(
            weights, fresh[slot][:, :LATENT_CHANNELS], preferred_element_type=jnp.float32
        )
        total = cache_total * shrink + jnp.sum(weights.astype(jnp.float32), axis=1, keepdims=True)
        out[slot] = (weighted / total).astype(jnp.bfloat16)


def finish(joined, queries, fresh, seq_here):
    own = joined.shape[1]
    row_start = seq_here * own
    own_queries = lax.dynamic_slice_in_dim(queries, row_start, own, 1)
    scores = (
        jnp.einsum("yeu,ynu->yen", own_queries, fresh, preferred_element_type=jnp.float32) * SCORE_SCALE
    )
    row_step = (row_start + jnp.arange(own, dtype=jnp.int32)) // HEADS
    col_step = jnp.arange(fresh.shape[1], dtype=jnp.int32)
    scores = jnp.where((col_step[None, :] <= row_step[:, None])[None], scores, NEG_FILL)
    return pl.pallas_call(
        finish_kernel,
        out_shape=jax.ShapeDtypeStruct((4, own, LATENT_CHANNELS), jnp.bfloat16),
        in_specs=[VMEM] * 3,
        out_specs=VMEM,
        compiler_params=params(),
        cost_estimate=pl.CostEstimate(flops=0, bytes_accessed=1 << 20, transcendentals=0),
        name="finish",
    )(scores, fresh, joined)


def tie(*xs):
    return lax.optimization_barrier(xs)


def over_seq(x):
    return lax.all_to_all(x, "seq", split_axis=0, concat_axis=0, tiled=True)


def all_along(x):
    return lax.all_to_all(x, "grp", split_axis=0, concat_axis=0, tiled=True)


def along(x, d):
    return lax.ppermute(x, "grp", [(i, (i + d) % 4) for i in range(4)])


def local(
    compressed,
    block_channel_scale,
    outlier_channels,
    outlier_values,
    lengths,
    assignment,
    padding,
    queries,
    decode_token_latent,
):
    group_here = lax.axis_index("grp")
    seq_here = lax.axis_index("seq")
    rows_here = [lax.dynamic_index_in_dim(x, group_here, 0, keepdims=False) for x in (lengths, assignment, padding)]
    place = jnp.stack([group_here, seq_here]).astype(jnp.int32)
    table = jnp.concatenate([place] + rows_here)
    packed = compressed.T
    channels = outlier_channels.T

    starts = [sum(CHUNKS[:i]) for i in range(len(CHUNKS))]
    last = len(CHUNKS) - 1
    latent = [
        dequantize(start, rows, place, lengths, padding, packed, block_channel_scale, channels, outlier_values)
        for start, rows in zip(starts, CHUNKS)
    ]
    turned = queries.transpose(0, 2, 1)
    latent[0], turned = tie(latent[0], turned)
    pieces = [along(x, d) for d, x in zip((1, 2, 3), split(table, turned))]
    handed = hand(table, turned, pieces)

    stripes, latent[1], handed, *pieces = tie(over_seq(latent[0]), latent[1], handed, *pieces)

    one, two, three, cache = pack(starts[0], table, stripes, None)
    following, one, two, three = tie(latent[1], one, two, three)
    one, two, three = along(one, 1), along(two, 2), along(three, 3)
    handed = lax.ppermute(handed, "seq", [(j, j ^ 1) for j in range(32)])
    partial = attend(table, turned, pieces, handed, latent)
    stripes, partial, *first = tie(over_seq(following), partial, one, two, three)

    one, two, three, cache = pack(starts[1], table, stripes, cache)
    partial, cache, one, two, three = tie(partial, cache, one, two, three)
    one, two, three = along(one, 1), along(two, 2), along(three, 3)
    cache = put(starts[0], table, (1, 2, 3), first, cache, later=True, cost=LONG)
    following, cache = tie(partial.reshape(32, 16, -1), cache)
    joined = all_along(join(table, over_seq(following)))
    cache = put(starts[1], table, (2,), (two,), cache)
    cache = put(starts[1], table, (1, 3), (one, three), cache)
    joined, cache = tie(joined, cache)
    attended = finish(joined, queries, decode_token_latent, seq_here)
    return cache.transpose(0, 1, 3, 2)[None, :, None], attended


def solution(mesh):
    placed = (
        P(("grp", "seq"), None),
        P(("grp", "seq"), None),
        P(("grp", "seq"), None),
        P(("grp", "seq"), None, None),
        P(),
        P(),
        P(),
        P("grp", None, None),
        P("grp", None, None),
    )
    return jax.shard_map(
        local,
        mesh=mesh,
        in_specs=placed,
        out_specs=(P("grp", None, "seq", None, None, None), P("grp", "seq", None)),
        check_vma=False,
    )
```

```python
import functools

import jax
import jax.numpy as jnp
from jax import lax
from jax.experimental import pallas as pl
from jax.experimental.pallas import tpu as pltpu
from jax.sharding import PartitionSpec as P

LATENT_CHANNELS = 512
MOST_STRIPES = 12
HEADS = 128
NEG_FILL = -1e30
SCORE_SCALE = 192.0 ** (-0.5)
CHUNKS = (272, 304)
KEY_TILE = 16
KEY_PART = 4
NOTE_LANES = 128

SMEM = pl.BlockSpec(memory_space=pltpu.SMEM)
HBM = pl.BlockSpec(memory_space=pltpu.HBM)
VMEM = pl.BlockSpec(memory_space=pltpu.VMEM)


LONG = pl.CostEstimate(flops=40 << 30, bytes_accessed=0, transcendentals=0)


def params(megabytes=16):
    return pltpu.CompilerParams(vmem_limit_bytes=megabytes << 20)


def moved(steps, rows):
    size = 2 * steps * MOST_STRIPES * rows * 128
    return pl.CostEstimate(flops=0, bytes_accessed=2 * size, transcendentals=0)


def request_for(table, target):
    first, count, before = 0, 0, 0
    for r in range(4):
        here = table[2 + r]
        hit = table[6 + r] == target
        first = jnp.where(hit, before, first)
        count = jnp.where(hit, here, count)
        before = before + here
    return first, count


def request_of(table, stripe):
    target, empty, before = 0, 0, 0
    for r in range(4):
        after = before + table[2 + r]
        inside = jnp.logical_and(stripe >= before, stripe < after)
        target = jnp.where(inside, table[6 + r], target)
        empty = jnp.where(stripe == after - 1, table[10 + r], empty)
        before = after
    return target, empty


def dequantize_kernel(start, per_step, total, lengths, padding, packed, scale, channels, values, out, scales, marks):
    rows = packed.shape[0]
    width = per_step * 16
    step = pl.program_id(0)

    @pl.when(step == 0)
    def _():
        mark = channels[...].astype(jnp.float32).T
        low, high = start // 128 * 128, min(-(-(start + rows) // 128) * 128, scale.shape[1])
        plain = scale[:, low:high]
        ids = (lax.broadcasted_iota(jnp.int32, plain.shape, 1) + low).astype(jnp.float32)
        for k in range(16):
            plain = jnp.where(ids == mark[:, k : k + 1], 0.0, plain)
        turned = plain.T[start - low : start - low + rows]
        for i in range(total):
            scales[i] = turned[:, i * per_step : (i + 1) * per_step]
            marks[i] = jnp.concatenate([mark[i * per_step + b : i * per_step + b + 1] for b in range(per_step)], axis=1)

    group, stripe = lax.axis_index("grp"), lax.axis_index("seq")
    empty, before = 0, 0
    for r in range(4):
        before = before + lengths[group, r]
        empty = jnp.where(stripe == before - 1, padding[group, r], empty)
    ids = (lax.broadcasted_iota(jnp.int32, (rows, width), 0) + start).astype(jnp.float32)
    onehot = (ids == marks[step]).astype(jnp.bfloat16)
    flat = values[...].reshape(width, 128)
    block = lax.broadcasted_iota(jnp.int32, (width, 128), 0) // 16
    spread = jnp.concatenate([jnp.where(block == b, flat, jnp.zeros_like(flat)) for b in range(per_step)], axis=1)
    outliers = jnp.dot(onehot, spread, preferred_element_type=jnp.float32)
    tokens = lax.broadcasted_iota(jnp.int32, (rows, 128), 1)
    here = scales[step]
    for b in range(per_step):
        lanes = slice(b * 128, (b + 1) * 128)
        latent = packed[:, lanes].astype(jnp.float32) * here[:, b : b + 1] + outliers[:, lanes]
        if b == per_step - 1:
            limit = jnp.where(step == total - 1, 128 - empty, 128)
            latent = jnp.where(tokens < limit, latent, 0.0)
        out[b] = latent.astype(jnp.bfloat16)


def dequantize(start, rows, lengths, padding, packed, scale, channels, values):
    packed, values = [pltpu.with_memory_space_constraint(x, pltpu.HBM) for x in (packed, values)]
    blocks = scale.shape[0]
    per_step = 16
    steps = blocks // per_step
    return pl.pallas_call(
        functools.partial(dequantize_kernel, start, per_step, steps),
        grid=(steps,),
        out_shape=pltpu.HBM((blocks, rows, 128), jnp.bfloat16),
        in_specs=[
            SMEM,
            SMEM,
            pl.BlockSpec((pl.Element(rows), pl.Element(per_step * 128)), lambda i: (start, i * per_step * 128)),
            pl.BlockSpec(scale.shape, lambda i: (0, 0)),
            pl.BlockSpec(channels.shape, lambda i: (0, 0)),
            pl.BlockSpec((per_step, 16, 128), lambda i: (i, 0, 0)),
        ],
        out_specs=pl.BlockSpec((per_step, rows, 128), lambda i: (i, 0, 0)),
        scratch_shapes=[
            pltpu.VMEM((steps, rows, per_step), jnp.float32),
            pltpu.VMEM((steps, 1, per_step * 16), jnp.float32),
        ],
        compiler_params=params(60),
        cost_estimate=pl.CostEstimate(flops=0, bytes_accessed=4 * blocks * rows * 128, transcendentals=0),
        name="dequantize",
    )(lengths, padding, packed, scale, channels, values)


def collect(table, d, stripes, target, zeros, sem):
    first, count = request_for(table, lax.rem(table[0] + d, 4))
    for v in range(MOST_STRIPES):

        @pl.when(v < count)
        def _():
            pltpu.make_async_copy(stripes.at[first + v], target.at[v], sem).start()

        @pl.when(v >= count)
        def _():
            pltpu.make_async_copy(zeros, target.at[v], sem).start()


def pack_kernel(start, table, stripes, *refs):
    *outs, cache, zeros, sems = refs[-6:]
    zeros[...] = jnp.zeros_like(zeros)
    targets = [cache.at[table[0], :, pl.ds(start, stripes.shape[1]), :], *outs]
    for d in (2, 1, 3, 0):
        collect(table, d, stripes, targets[d], zeros, sems.at[d])
    for d, target in enumerate(targets):
        pltpu.make_async_copy(target, target, sems.at[d]).wait()


def pack(start, table, stripes, cache):
    rows = stripes.shape[1]
    more = () if cache is None else (cache,)
    one = pltpu.HBM((MOST_STRIPES, rows, 128), jnp.bfloat16)
    return pl.pallas_call(
        functools.partial(pack_kernel, start),
        out_shape=(one, one, one, jax.ShapeDtypeStruct((4, MOST_STRIPES, sum(CHUNKS), 128), jnp.bfloat16)),
        in_specs=[SMEM, VMEM] + [HBM] * len(more),
        out_specs=(HBM,) * 4,
        input_output_aliases={2: 3} if more else {},
        scratch_shapes=[pltpu.VMEM((rows, 128), jnp.bfloat16), pltpu.SemaphoreType.DMA((4,))],
        compiler_params=params(),
        cost_estimate=moved(4, rows),
        name="pack",
    )(table, stripes, *more)


PIECES = 3


def put_copies(start, steps, table, arrived, out, sems):
    rows, size = arrived[0].shape[1], MOST_STRIPES // PIECES
    copies = []
    for i, d in enumerate(steps):
        slot = out.at[lax.rem(table[0] + 4 - d, 4)]
        for h in range(PIECES):
            part = pl.ds(h * size, size)
            copies.append(
                pltpu.make_async_copy(arrived[i].at[part], slot.at[part, pl.ds(start, rows), :], sems.at[i, h])
            )
    return copies


def put_kernel(start, steps, table, *refs):
    arrived, (out, sems) = refs[: len(steps)], refs[-2:]
    copies = put_copies(start, steps, table, arrived, out, sems)
    for copy in copies:
        copy.start()
    for copy in copies:
        copy.wait()


def put_later_kernel(start, steps, table, *refs):
    arrived, (out, sems, held, in_sems) = refs[: len(steps)], refs[-4:]
    come = [pltpu.make_async_copy(arrived[i], held.at[i], in_sems.at[i]) for i in range(len(steps))]
    leave = put_copies(start, steps, table, [held.at[i] for i in range(len(steps))], out, sems)
    for copy in come:
        copy.start()
    for i, copy in enumerate(come):
        copy.wait()
        for part in leave[i * PIECES : (i + 1) * PIECES]:
            part.start()
    for part in leave:
        part.wait()


def put(start, table, steps, arrived, cache, later=False, cost=None):
    rows = arrived[0].shape[1]
    scratch = [pltpu.SemaphoreType.DMA((len(steps), PIECES))]
    if later:
        scratch += [
            pltpu.VMEM((len(steps), MOST_STRIPES, rows, 128), jnp.bfloat16),
            pltpu.SemaphoreType.DMA((len(steps),)),
        ]
    return pl.pallas_call(
        functools.partial(put_later_kernel if later else put_kernel, start, steps),
        out_shape=jax.ShapeDtypeStruct((4, MOST_STRIPES, sum(CHUNKS), 128), jnp.bfloat16),
        in_specs=[SMEM] + [pl.BlockSpec(memory_space=pl.ANY) if later else VMEM] * len(steps) + [HBM],
        out_specs=HBM,
        input_output_aliases={len(steps) + 1: 0},
        scratch_shapes=scratch,
        compiler_params=params(),
        cost_estimate=cost or moved(len(steps), rows),
        name="put",
    )(table, *arrived, cache)


def partner(table):
    return table[1] + 1 - 2 * lax.rem(table[1], 2)


def half_of(table, rows):
    return pl.ds(pl.multiple_of(lax.rem(table[1], 2) * rows, rows), rows)


def split_kernel(table, queries, *refs):
    outs, (held, in_sems, out_sems) = refs[:3], refs[3:]
    half = half_of(table, held.shape[1])
    come = [
        pltpu.make_async_copy(queries.at[lax.rem(table[0] + d + 1, 4), half], held.at[d], in_sems.at[d])
        for d in range(3)
    ]
    leave = [pltpu.make_async_copy(held.at[d], outs[d], out_sems.at[d]) for d in range(3)]
    for copy in come:
        copy.start()
    for d in range(3):
        come[d].wait()
        leave[d].start()
    for copy in leave:
        copy.wait()


def split(table, queries):
    shape = (queries.shape[1] // 2, queries.shape[2])
    return pl.pallas_call(
        split_kernel,
        out_shape=(pltpu.HBM(shape, queries.dtype),) * 3,
        in_specs=[SMEM, HBM],
        out_specs=(HBM,) * 3,
        scratch_shapes=[
            pltpu.VMEM((3,) + shape, queries.dtype),
            pltpu.SemaphoreType.DMA((3,)),
            pltpu.SemaphoreType.DMA((3,)),
        ],
        compiler_params=params(),
        cost_estimate=pl.CostEstimate(flops=0, bytes_accessed=1 << 20, transcendentals=0),
        name="split",
    )(table, pltpu.with_memory_space_constraint(queries, pltpu.HBM))


def start_half(table, target, queries, pieces, out, sem):
    for d in range(4):
        source = queries.at[table[0], half_of(table, out.shape[0])] if d == 0 else pieces[d - 1]

        @pl.when(target == lax.rem(table[0] + 4 - d, 4))
        def _():
            pltpu.make_async_copy(source, out, sem).start()


def hand_kernel(table, queries, in1, in2, in3, out, sem):
    target, _ = request_of(table, partner(table))
    start_half(table, target, queries, (in1, in2, in3), out, sem)
    pltpu.make_async_copy(in1, out, sem).wait()


def hand(table, queries, pieces):
    queries = pltpu.with_memory_space_constraint(queries, pltpu.HBM)
    return pl.pallas_call(
        hand_kernel,
        out_shape=jax.ShapeDtypeStruct(pieces[0].shape, pieces[0].dtype),
        in_specs=[SMEM, HBM] + [VMEM] * 3,
        out_specs=VMEM,
        scratch_shapes=[pltpu.SemaphoreType.DMA],
        compiler_params=params(),
        cost_estimate=pl.CostEstimate(flops=0, bytes_accessed=1 << 20, transcendentals=0),
        name="hand",
    )(table, queries, *pieces)


def in_three(x):
    high = x.astype(jnp.bfloat16)
    rest = x - high.astype(jnp.float32)
    middle = rest.astype(jnp.bfloat16)
    low = (rest - middle.astype(jnp.float32)).astype(jnp.bfloat16)
    return high, middle, low


def attend_kernel(steps, table, *refs):
    sources, handed, keys = refs[:4], refs[4], refs[5 : 5 + len(CHUNKS)]
    out, peak, total, weighted, turned, queries, sems = refs[5 + len(CHUNKS) :]
    step = pl.program_id(0)
    target, empty = request_of(table, table[1])

    @pl.when(step == 0)
    def _():
        rows = handed.shape[0]
        mine, other = turned.at[half_of(table, rows)], turned.at[half_of((0, partner(table)), rows)]
        start_half(table, target, sources[0], sources[1:], mine, sems.at[0])
        copy = pltpu.make_async_copy(handed, other, sems.at[1])
        copy.start()
        copy.wait()
        pltpu.make_async_copy(sources[1], mine, sems.at[0]).wait()
        queries[...] = turned[...].T
        peak[...] = jnp.full_like(peak, NEG_FILL)
        total[...] = jnp.zeros_like(total)
        weighted[...] = jnp.zeros_like(weighted)

    parts = [
        jnp.concatenate(
            [jnp.concatenate([k[b] for k in keys], axis=0) for b in range(i, i + KEY_PART)], axis=1
        )
        for i in range(0, KEY_TILE, KEY_PART)
    ]
    scores = [jnp.dot(queries[...], part, preferred_element_type=jnp.float32) for part in parts]
    limit = jnp.where(step == steps - 1, KEY_PART * 128 - empty, KEY_PART * 128)
    columns = lax.broadcasted_iota(jnp.int32, (1, KEY_PART * 128), 1)
    scores[-1] = scores[-1] + jnp.where(columns < limit, 0.0, NEG_FILL)
    before = peak[...]
    now = before
    for score in scores:
        now = jnp.maximum(now, jnp.max(score, axis=1, keepdims=True))
    shrink = jnp.exp((before - now) * SCORE_SCALE)
    whole, sums = total[...] * shrink, weighted[...] * shrink[:, :1]
    for score, part in zip(scores, parts):
        weights = jnp.exp((score - now[:, :1]) * SCORE_SCALE).astype(jnp.bfloat16)
        whole = whole + jnp.sum(weights.astype(jnp.float32), axis=1, keepdims=True)
        sums = sums + lax.dot_general(
            weights, part[:LATENT_CHANNELS], (((1,), (1,)), ((), ())), preferred_element_type=jnp.float32
        )
    total[...], weighted[...], peak[...] = whole, sums, now

    @pl.when(step == steps - 1)
    def _():
        out[:, :LATENT_CHANNELS] = weighted[...].astype(jnp.bfloat16)
        lane = lax.broadcasted_iota(jnp.int32, peak.shape, 1)
        note = jnp.zeros(peak.shape, jnp.float32)
        for i, part in enumerate(in_three(peak[...] * SCORE_SCALE) + in_three(total[...])):
            note = jnp.where(lane == i, part.astype(jnp.float32), note)
        out[:, LATENT_CHANNELS:] = note.astype(jnp.bfloat16)


def attend(table, queries, pieces, handed, keys):
    channels, rows = queries.shape[1:]
    queries = pltpu.with_memory_space_constraint(queries, pltpu.HBM)
    keys = [pltpu.with_memory_space_constraint(k, pltpu.HBM) for k in keys]
    blocks = keys[0].shape[0]
    steps = blocks // KEY_TILE
    width = LATENT_CHANNELS + NOTE_LANES
    return pl.pallas_call(
        functools.partial(attend_kernel, steps),
        grid=(steps,),
        out_shape=pltpu.HBM((rows, width), jnp.bfloat16),
        in_specs=[SMEM, HBM] + [VMEM] * 4
        + [pl.BlockSpec((KEY_TILE,) + k.shape[1:], lambda i: (i, 0, 0)) for k in keys],
        out_specs=pl.BlockSpec((rows, width), lambda i: (0, 0)),
        scratch_shapes=[
            pltpu.VMEM((rows, 128), jnp.float32),
            pltpu.VMEM((rows, 128), jnp.float32),
            pltpu.VMEM((rows, LATENT_CHANNELS), jnp.float32),
            pltpu.VMEM((channels, rows), jnp.bfloat16),
            pltpu.VMEM((rows, channels), jnp.bfloat16),
            pltpu.SemaphoreType.DMA((2,)),
        ],
        compiler_params=params(44),
        cost_estimate=LONG,
        name="attend",
    )(table, queries, *pieces, handed, *keys)


def join_kernel(table, partials, out):
    stripes, rows, _ = partials.shape
    note = partials[:, :, LATENT_CHANNELS:].astype(jnp.float32)
    peak = note[:, :, 0:1] + note[:, :, 1:2] + note[:, :, 2:3]
    total = note[:, :, 3:4] + note[:, :, 4:5] + note[:, :, 5:6]
    stripe = lax.broadcasted_iota(jnp.int32, peak.shape, 0)
    lane = lax.broadcasted_iota(jnp.int32, (rows, NOTE_LANES), 1)
    values = partials[:, :, :LATENT_CHANNELS].astype(jnp.float32)
    for d in range(4):
        first, count = request_for(table, d)
        inside = jnp.logical_and(stripe >= first, stripe < first + count)
        top = jnp.max(jnp.where(inside, peak, NEG_FILL), axis=0)
        factor = jnp.where(inside, jnp.exp(jnp.where(inside, peak, NEG_FILL) - top[None]), 0.0)
        out[d, :, :LATENT_CHANNELS] = jnp.sum(values * factor, axis=0)
        whole = jnp.sum(total * factor, axis=0)
        out[d, :, LATENT_CHANNELS:] = jnp.where(lane == 0, top, jnp.where(lane == 1, whole, 0.0))


def join(table, partials):
    return pl.pallas_call(
        join_kernel,
        out_shape=jax.ShapeDtypeStruct((4,) + partials.shape[1:], jnp.float32),
        in_specs=[SMEM, VMEM],
        out_specs=VMEM,
        compiler_params=params(),
        cost_estimate=pl.CostEstimate(flops=0, bytes_accessed=1 << 20, transcendentals=0),
        name="join",
    )(table, partials)


def finish_kernel(scores, fresh, joined, out):
    for slot in range(4):
        cache_peak = joined[slot, :, LATENT_CHANNELS : LATENT_CHANNELS + 1]
        cache_total = joined[slot, :, LATENT_CHANNELS + 1 : LATENT_CHANNELS + 2]
        peak = jnp.maximum(cache_peak, jnp.max(scores[slot], axis=1, keepdims=True))
        shrink = jnp.exp(cache_peak - peak)
        weights = jnp.exp(scores[slot] - peak).astype(jnp.bfloat16)
        weighted = joined[slot, :, :LATENT_CHANNELS] * shrink + jnp.dot(
            weights, fresh[slot][:, :LATENT_CHANNELS], preferred_element_type=jnp.float32
        )
        total = cache_total * shrink + jnp.sum(weights.astype(jnp.float32), axis=1, keepdims=True)
        out[slot] = (weighted / total).astype(jnp.bfloat16)


def finish(joined, queries, fresh, seq_here):
    own = joined.shape[1]
    row_start = seq_here * own
    own_queries = lax.dynamic_slice_in_dim(queries, row_start, own, 1)
    scores = (
        jnp.einsum("yeu,ynu->yen", own_queries, fresh, preferred_element_type=jnp.float32) * SCORE_SCALE
    )
    row_step = (row_start + jnp.arange(own, dtype=jnp.int32)) // HEADS
    col_step = jnp.arange(fresh.shape[1], dtype=jnp.int32)
    scores = jnp.where((col_step[None, :] <= row_step[:, None])[None], scores, NEG_FILL)
    return pl.pallas_call(
        finish_kernel,
        out_shape=jax.ShapeDtypeStruct((4, own, LATENT_CHANNELS), jnp.bfloat16),
        in_specs=[VMEM] * 3,
        out_specs=VMEM,
        compiler_params=params(),
        cost_estimate=pl.CostEstimate(flops=0, bytes_accessed=1 << 20, transcendentals=0),
        name="finish",
    )(scores, fresh, joined)


def tie(*xs):
    return lax.optimization_barrier(xs)


def over_seq(x):
    return lax.all_to_all(x, "seq", split_axis=0, concat_axis=0, tiled=True)


def all_along(x):
    return lax.all_to_all(x, "grp", split_axis=0, concat_axis=0, tiled=True)


def along(x, d):
    return lax.ppermute(x, "grp", [(i, (i + d) % 4) for i in range(4)])


def local(
    compressed,
    block_channel_scale,
    outlier_channels,
    outlier_values,
    lengths,
    assignment,
    padding,
    queries,
    decode_token_latent,
):
    group_here = lax.axis_index("grp")
    seq_here = lax.axis_index("seq")
    rows_here = [lax.dynamic_index_in_dim(x, group_here, 0, keepdims=False) for x in (lengths, assignment, padding)]
    place = jnp.stack([group_here, seq_here]).astype(jnp.int32)
    table = jnp.concatenate([place] + rows_here)
    packed = compressed.T
    channels = outlier_channels.T

    starts = [sum(CHUNKS[:i]) for i in range(len(CHUNKS))]
    last = len(CHUNKS) - 1
    latent = [
        dequantize(start, rows, lengths, padding, packed, block_channel_scale, channels, outlier_values)
        for start, rows in zip(starts, CHUNKS)
    ]
    turned = queries.transpose(0, 2, 1)
    latent[0], turned = tie(latent[0], turned)
    pieces = [along(x, d) for d, x in zip((1, 2, 3), split(table, turned))]
    handed = hand(table, turned, pieces)

    stripes, latent[1], handed, *pieces = tie(over_seq(latent[0]), latent[1], handed, *pieces)

    one, two, three, cache = pack(starts[0], table, stripes, None)
    following, one, two, three = tie(latent[1], one, two, three)
    one, two, three = along(one, 1), along(two, 2), along(three, 3)
    handed = lax.ppermute(handed, "seq", [(j, j ^ 1) for j in range(32)])
    partial = attend(table, turned, pieces, handed, latent)
    stripes, partial, *first = tie(over_seq(following), partial, one, two, three)

    one, two, three, cache = pack(starts[1], table, stripes, cache)
    partial, cache, one, two, three = tie(partial, cache, one, two, three)
    one, two, three = along(one, 1), along(two, 2), along(three, 3)
    cache = put(starts[0], table, (1, 2, 3), first, cache, later=True, cost=LONG)
    following, cache = tie(partial.reshape(32, 16, -1), cache)
    joined = all_along(join(table, over_seq(following)))
    cache = put(starts[1], table, (2,), (two,), cache)
    cache = put(starts[1], table, (1, 3), (one, three), cache)
    joined, cache = tie(joined, cache)
    attended = finish(joined, queries, decode_token_latent, seq_here)
    return cache.transpose(0, 1, 3, 2)[None, :, None], attended


def solution(mesh):
    placed = (
        P(("grp", "seq"), None),
        P(("grp", "seq"), None),
        P(("grp", "seq"), None),
        P(("grp", "seq"), None, None),
        P(),
        P(),
        P(),
        P("grp", None, None),
        P("grp", None, None),
    )
    return jax.shard_map(
        local,
        mesh=mesh,
        in_specs=placed,
        out_specs=(P("grp", None, "seq", None, None, None), P("grp", "seq", None)),
        check_vma=False,
    )
```

```python
import functools

import jax
import jax.numpy as jnp
from jax import lax
from jax.experimental import pallas as pl
from jax.experimental.pallas import tpu as pltpu
from jax.sharding import PartitionSpec as P

LATENT_CHANNELS = 512
MOST_STRIPES = 12
HEADS = 128
NEG_FILL = -1e30
SCORE_SCALE = 192.0 ** (-0.5)
CHUNKS = (272, 304)
KEY_TILE = 16
KEY_PART = 4
NOTE_LANES = 128

SMEM = pl.BlockSpec(memory_space=pltpu.SMEM)
HBM = pl.BlockSpec(memory_space=pltpu.HBM)
VMEM = pl.BlockSpec(memory_space=pltpu.VMEM)


LONG = pl.CostEstimate(flops=40 << 30, bytes_accessed=0, transcendentals=0)


def params(megabytes=16):
    return pltpu.CompilerParams(vmem_limit_bytes=megabytes << 20)


def moved(steps, rows):
    size = 2 * steps * MOST_STRIPES * rows * 128
    return pl.CostEstimate(flops=0, bytes_accessed=2 * size, transcendentals=0)


def request_for(table, target):
    first, count, before = 0, 0, 0
    for r in range(4):
        here = table[2 + r]
        hit = table[6 + r] == target
        first = jnp.where(hit, before, first)
        count = jnp.where(hit, here, count)
        before = before + here
    return first, count


def request_of(table, stripe):
    target, empty, before = 0, 0, 0
    for r in range(4):
        after = before + table[2 + r]
        inside = jnp.logical_and(stripe >= before, stripe < after)
        target = jnp.where(inside, table[6 + r], target)
        empty = jnp.where(stripe == after - 1, table[10 + r], empty)
        before = after
    return target, empty


def dequantize_kernel(start, per_step, total, lengths, padding, packed, scale, channels, values, out, scales, marks):
    rows = packed.shape[0]
    width = per_step * 16
    step = pl.program_id(0)

    @pl.when(step == 0)
    def _():
        mark = channels[...].astype(jnp.float32).T
        low, high = start // 128 * 128, min(-(-(start + rows) // 128) * 128, scale.shape[1])
        plain = scale[:, low:high]
        ids = (lax.broadcasted_iota(jnp.int32, plain.shape, 1) + low).astype(jnp.float32)
        for k in range(16):
            plain = jnp.where(ids == mark[:, k : k + 1], 0.0, plain)
        turned = plain.T[start - low : start - low + rows]
        for i in range(total):
            scales[i] = turned[:, i * per_step : (i + 1) * per_step]
            marks[i] = jnp.concatenate([mark[i * per_step + b : i * per_step + b + 1] for b in range(per_step)], axis=1)

    group, stripe = lax.axis_index("grp"), lax.axis_index("seq")
    empty, before = 0, 0
    for r in range(4):
        before = before + lengths[group, r]
        empty = jnp.where(stripe == before - 1, padding[group, r], empty)
    ids = (lax.broadcasted_iota(jnp.int32, (rows, width), 0) + start).astype(jnp.float32)
    onehot = (ids == marks[step]).astype(jnp.bfloat16)
    flat = values[...].reshape(width, 128)
    block = lax.broadcasted_iota(jnp.int32, (width, 128), 0) // 16
    spread = jnp.concatenate([jnp.where(block == b, flat, jnp.zeros_like(flat)) for b in range(per_step)], axis=1)
    outliers = jnp.dot(onehot, spread, preferred_element_type=jnp.float32)
    tokens = lax.broadcasted_iota(jnp.int32, (rows, 128), 1)
    here = scales[step]
    for b in range(per_step):
        lanes = slice(b * 128, (b + 1) * 128)
        latent = packed[:, lanes].astype(jnp.float32) * here[:, b : b + 1] + outliers[:, lanes]
        if b == per_step - 1:
            limit = jnp.where(step == total - 1, 128 - empty, 128)
            latent = jnp.where(tokens < limit, latent, 0.0)
        out[b] = latent.astype(jnp.bfloat16)


def dequantize(start, rows, lengths, padding, packed, scale, channels, values):
    packed, values = [pltpu.with_memory_space_constraint(x, pltpu.HBM) for x in (packed, values)]
    blocks = scale.shape[0]
    per_step = 16
    steps = blocks // per_step
    return pl.pallas_call(
        functools.partial(dequantize_kernel, start, per_step, steps),
        grid=(steps,),
        out_shape=pltpu.HBM((blocks, rows, 128), jnp.bfloat16),
        in_specs=[
            SMEM,
            SMEM,
            pl.BlockSpec((pl.Element(rows), pl.Element(per_step * 128)), lambda i: (start, i * per_step * 128)),
            pl.BlockSpec(scale.shape, lambda i: (0, 0)),
            pl.BlockSpec(channels.shape, lambda i: (0, 0)),
            pl.BlockSpec((per_step, 16, 128), lambda i: (i, 0, 0)),
        ],
        out_specs=pl.BlockSpec((per_step, rows, 128), lambda i: (i, 0, 0)),
        scratch_shapes=[
            pltpu.VMEM((steps, rows, per_step), jnp.float32),
            pltpu.VMEM((steps, 1, per_step * 16), jnp.float32),
        ],
        compiler_params=params(60),
        cost_estimate=pl.CostEstimate(flops=0, bytes_accessed=4 * blocks * rows * 128, transcendentals=0),
        name="dequantize",
    )(lengths, padding, packed, scale, channels, values)


def collect(table, d, stripes, target, zeros, sem):
    first, count = request_for(table, lax.rem(table[0] + d, 4))
    for v in range(MOST_STRIPES):

        @pl.when(v < count)
        def _():
            pltpu.make_async_copy(stripes.at[first + v], target.at[v], sem).start()

        @pl.when(v >= count)
        def _():
            pltpu.make_async_copy(zeros, target.at[v], sem).start()


def pack_kernel(start, table, stripes, *refs):
    *outs, cache, zeros, sems = refs[-6:]
    zeros[...] = jnp.zeros_like(zeros)
    targets = [cache.at[table[0], :, pl.ds(start, stripes.shape[1]), :], *outs]
    for d in (2, 1, 3, 0):
        collect(table, d, stripes, targets[d], zeros, sems.at[d])
    for d, target in enumerate(targets):
        pltpu.make_async_copy(target, target, sems.at[d]).wait()


def pack(start, table, stripes, cache):
    rows = stripes.shape[1]
    more = () if cache is None else (cache,)
    one = pltpu.HBM((MOST_STRIPES, rows, 128), jnp.bfloat16)
    return pl.pallas_call(
        functools.partial(pack_kernel, start),
        out_shape=(one, one, one, jax.ShapeDtypeStruct((4, MOST_STRIPES, sum(CHUNKS), 128), jnp.bfloat16)),
        in_specs=[SMEM, VMEM] + [HBM] * len(more),
        out_specs=(HBM,) * 4,
        input_output_aliases={2: 3} if more else {},
        scratch_shapes=[pltpu.VMEM((rows, 128), jnp.bfloat16), pltpu.SemaphoreType.DMA((4,))],
        compiler_params=params(),
        cost_estimate=moved(4, rows),
        name="pack",
    )(table, stripes, *more)


PIECES = 3


def put_copies(start, steps, table, arrived, out, sems):
    rows, size = arrived[0].shape[1], MOST_STRIPES // PIECES
    copies = []
    for i, d in enumerate(steps):
        slot = out.at[lax.rem(table[0] + 4 - d, 4)]
        for h in range(PIECES):
            part = pl.ds(h * size, size)
            copies.append(
                pltpu.make_async_copy(arrived[i].at[part], slot.at[part, pl.ds(start, rows), :], sems.at[i, h])
            )
    return copies


def put_kernel(start, steps, table, *refs):
    arrived, (out, sems) = refs[: len(steps)], refs[-2:]
    copies = put_copies(start, steps, table, arrived, out, sems)
    for copy in copies:
        copy.start()
    for copy in copies:
        copy.wait()


def put_later_kernel(start, steps, table, *refs):
    arrived, (out, sems, held, in_sems) = refs[: len(steps)], refs[-4:]
    come = [pltpu.make_async_copy(arrived[i], held.at[i], in_sems.at[i]) for i in range(len(steps))]
    leave = put_copies(start, steps, table, [held.at[i] for i in range(len(steps))], out, sems)
    for copy in come:
        copy.start()
    for i, copy in enumerate(come):
        copy.wait()
        for part in leave[i * PIECES : (i + 1) * PIECES]:
            part.start()
    for part in leave:
        part.wait()


def put(start, table, steps, arrived, cache, later=False, cost=None):
    rows = arrived[0].shape[1]
    scratch = [pltpu.SemaphoreType.DMA((len(steps), PIECES))]
    if later:
        scratch += [
            pltpu.VMEM((len(steps), MOST_STRIPES, rows, 128), jnp.bfloat16),
            pltpu.SemaphoreType.DMA((len(steps),)),
        ]
    return pl.pallas_call(
        functools.partial(put_later_kernel if later else put_kernel, start, steps),
        out_shape=jax.ShapeDtypeStruct((4, MOST_STRIPES, sum(CHUNKS), 128), jnp.bfloat16),
        in_specs=[SMEM] + [pl.BlockSpec(memory_space=pl.ANY) if later else VMEM] * len(steps) + [HBM],
        out_specs=HBM,
        input_output_aliases={len(steps) + 1: 0},
        scratch_shapes=scratch,
        compiler_params=params(),
        cost_estimate=cost or moved(len(steps), rows),
        name="put",
    )(table, *arrived, cache)


def partner(table):
    return table[1] + 1 - 2 * lax.rem(table[1], 2)


def half_of(table, rows):
    return pl.ds(pl.multiple_of(lax.rem(table[1], 2) * rows, rows), rows)


def split_kernel(table, queries, *refs):
    outs, (held, in_sems, out_sems) = refs[:3], refs[3:]
    half = half_of(table, held.shape[1])
    come = [
        pltpu.make_async_copy(queries.at[lax.rem(table[0] + d + 1, 4), half], held.at[d], in_sems.at[d])
        for d in range(3)
    ]
    leave = [pltpu.make_async_copy(held.at[d], outs[d], out_sems.at[d]) for d in range(3)]
    for copy in come:
        copy.start()
    for d in range(3):
        come[d].wait()
        leave[d].start()
    for copy in leave:
        copy.wait()


def split(table, queries):
    shape = (queries.shape[1] // 2, queries.shape[2])
    return pl.pallas_call(
        split_kernel,
        out_shape=(pltpu.HBM(shape, queries.dtype),) * 3,
        in_specs=[SMEM, HBM],
        out_specs=(HBM,) * 3,
        scratch_shapes=[
            pltpu.VMEM((3,) + shape, queries.dtype),
            pltpu.SemaphoreType.DMA((3,)),
            pltpu.SemaphoreType.DMA((3,)),
        ],
        compiler_params=params(),
        cost_estimate=pl.CostEstimate(flops=0, bytes_accessed=1 << 20, transcendentals=0),
        name="split",
    )(table, pltpu.with_memory_space_constraint(queries, pltpu.HBM))


def start_half(table, target, queries, pieces, out, sem):
    for d in range(4):
        source = queries.at[table[0], half_of(table, out.shape[0])] if d == 0 else pieces[d - 1]

        @pl.when(target == lax.rem(table[0] + 4 - d, 4))
        def _():
            pltpu.make_async_copy(source, out, sem).start()


def hand_kernel(table, queries, in1, in2, in3, out, sem):
    target, _ = request_of(table, partner(table))
    start_half(table, target, queries, (in1, in2, in3), out, sem)
    pltpu.make_async_copy(in1, out, sem).wait()


def hand(table, queries, pieces):
    queries = pltpu.with_memory_space_constraint(queries, pltpu.HBM)
    return pl.pallas_call(
        hand_kernel,
        out_shape=jax.ShapeDtypeStruct(pieces[0].shape, pieces[0].dtype),
        in_specs=[SMEM, HBM] + [VMEM] * 3,
        out_specs=VMEM,
        scratch_shapes=[pltpu.SemaphoreType.DMA],
        compiler_params=params(),
        cost_estimate=pl.CostEstimate(flops=0, bytes_accessed=1 << 20, transcendentals=0),
        name="hand",
    )(table, queries, *pieces)


def in_three(x):
    high = x.astype(jnp.bfloat16)
    rest = x - high.astype(jnp.float32)
    middle = rest.astype(jnp.bfloat16)
    low = (rest - middle.astype(jnp.float32)).astype(jnp.bfloat16)
    return high, middle, low


def attend_kernel(steps, table, *refs):
    sources, handed, keys = refs[:4], refs[4], refs[5 : 5 + len(CHUNKS)]
    out, peak, total, weighted, turned, queries, sems = refs[5 + len(CHUNKS) :]
    step = pl.program_id(0)
    target, empty = request_of(table, table[1])

    @pl.when(step == 0)
    def _():
        rows = handed.shape[0]
        mine, other = turned.at[half_of(table, rows)], turned.at[half_of((0, partner(table)), rows)]
        start_half(table, target, sources[0], sources[1:], mine, sems.at[0])
        copy = pltpu.make_async_copy(handed, other, sems.at[1])
        copy.start()
        copy.wait()
        pltpu.make_async_copy(sources[1], mine, sems.at[0]).wait()
        queries[...] = turned[...].T
        peak[...] = jnp.full_like(peak, NEG_FILL)
        total[...] = jnp.zeros_like(total)
        weighted[...] = jnp.zeros_like(weighted)

    parts = [
        jnp.concatenate(
            [jnp.concatenate([k[b] for k in keys], axis=0) for b in range(i, i + KEY_PART)], axis=1
        )
        for i in range(0, KEY_TILE, KEY_PART)
    ]
    scores = [jnp.dot(queries[...], part, preferred_element_type=jnp.float32) for part in parts]
    limit = jnp.where(step == steps - 1, KEY_PART * 128 - empty, KEY_PART * 128)
    columns = lax.broadcasted_iota(jnp.int32, (1, KEY_PART * 128), 1)
    scores[-1] = scores[-1] + jnp.where(columns < limit, 0.0, NEG_FILL)
    before = peak[...]
    now = before
    for score in scores:
        now = jnp.maximum(now, jnp.max(score, axis=1, keepdims=True))
    shrink = jnp.exp((before - now) * SCORE_SCALE)
    whole, sums = total[...] * shrink, weighted[...] * shrink[:, :1]
    for score, part in zip(scores, parts):
        weights = jnp.exp((score - now[:, :1]) * SCORE_SCALE).astype(jnp.bfloat16)
        whole = whole + jnp.sum(weights.astype(jnp.float32), axis=1, keepdims=True)
        sums = sums + lax.dot_general(
            weights, part[:LATENT_CHANNELS], (((1,), (1,)), ((), ())), preferred_element_type=jnp.float32
        )
    total[...], weighted[...], peak[...] = whole, sums, now

    @pl.when(step == steps - 1)
    def _():
        out[:, :LATENT_CHANNELS] = weighted[...].astype(jnp.bfloat16)
        lane = lax.broadcasted_iota(jnp.int32, peak.shape, 1)
        note = jnp.zeros(peak.shape, jnp.float32)
        for i, part in enumerate(in_three(peak[...] * SCORE_SCALE) + in_three(total[...])):
            note = jnp.where(lane == i, part.astype(jnp.float32), note)
        out[:, LATENT_CHANNELS:] = note.astype(jnp.bfloat16)


def attend(table, queries, pieces, handed, keys):
    channels, rows = queries.shape[1:]
    queries = pltpu.with_memory_space_constraint(queries, pltpu.HBM)
    keys = [pltpu.with_memory_space_constraint(k, pltpu.HBM) for k in keys]
    blocks = keys[0].shape[0]
    steps = blocks // KEY_TILE
    width = LATENT_CHANNELS + NOTE_LANES
    return pl.pallas_call(
        functools.partial(attend_kernel, steps),
        grid=(steps,),
        out_shape=pltpu.HBM((rows, width), jnp.bfloat16),
        in_specs=[SMEM, HBM] + [VMEM] * 4
        + [pl.BlockSpec((KEY_TILE,) + k.shape[1:], lambda i: (i, 0, 0)) for k in keys],
        out_specs=pl.BlockSpec((rows, width), lambda i: (0, 0)),
        scratch_shapes=[
            pltpu.VMEM((rows, 128), jnp.float32),
            pltpu.VMEM((rows, 128), jnp.float32),
            pltpu.VMEM((rows, LATENT_CHANNELS), jnp.float32),
            pltpu.VMEM((channels, rows), jnp.bfloat16),
            pltpu.VMEM((rows, channels), jnp.bfloat16),
            pltpu.SemaphoreType.DMA((2,)),
        ],
        compiler_params=params(44),
        cost_estimate=LONG,
        name="attend",
    )(table, queries, *pieces, handed, *keys)


def join_kernel(table, partials, out):
    stripes, rows, _ = partials.shape
    note = partials[:, :, LATENT_CHANNELS:].astype(jnp.float32)
    peak = note[:, :, 0:1] + note[:, :, 1:2] + note[:, :, 2:3]
    total = note[:, :, 3:4] + note[:, :, 4:5] + note[:, :, 5:6]
    stripe = lax.broadcasted_iota(jnp.int32, peak.shape, 0)
    lane = lax.broadcasted_iota(jnp.int32, (rows, NOTE_LANES), 1)
    values = partials[:, :, :LATENT_CHANNELS].astype(jnp.float32)
    for d in range(4):
        first, count = request_for(table, d)
        inside = jnp.logical_and(stripe >= first, stripe < first + count)
        top = jnp.max(jnp.where(inside, peak, NEG_FILL), axis=0)
        factor = jnp.where(inside, jnp.exp(jnp.where(inside, peak, NEG_FILL) - top[None]), 0.0)
        out[d, :, :LATENT_CHANNELS] = jnp.sum(values * factor, axis=0)
        whole = jnp.sum(total * factor, axis=0)
        out[d, :, LATENT_CHANNELS:] = jnp.where(lane == 0, top, jnp.where(lane == 1, whole, 0.0))


def join(table, partials):
    return pl.pallas_call(
        join_kernel,
        out_shape=jax.ShapeDtypeStruct((4,) + partials.shape[1:], jnp.float32),
        in_specs=[SMEM, VMEM],
        out_specs=VMEM,
        compiler_params=params(),
        cost_estimate=pl.CostEstimate(flops=0, bytes_accessed=1 << 20, transcendentals=0),
        name="join",
    )(table, partials)


def finish_kernel(scores, fresh, joined, out):
    for slot in range(4):
        cache_peak = joined[slot, :, LATENT_CHANNELS : LATENT_CHANNELS + 1]
        cache_total = joined[slot, :, LATENT_CHANNELS + 1 : LATENT_CHANNELS + 2]
        peak = jnp.maximum(cache_peak, jnp.max(scores[slot], axis=1, keepdims=True))
        shrink = jnp.exp(cache_peak - peak)
        weights = jnp.exp(scores[slot] - peak).astype(jnp.bfloat16)
        weighted = joined[slot, :, :LATENT_CHANNELS] * shrink + jnp.dot(
            weights, fresh[slot][:, :LATENT_CHANNELS], preferred_element_type=jnp.float32
        )
        total = cache_total * shrink + jnp.sum(weights.astype(jnp.float32), axis=1, keepdims=True)
        out[slot] = (weighted / total).astype(jnp.bfloat16)


def finish(joined, queries, fresh, seq_here):
    own = joined.shape[1]
    row_start = seq_here * own
    own_queries = lax.dynamic_slice_in_dim(queries, row_start, own, 1)
    scores = (
        jnp.einsum("yeu,ynu->yen", own_queries, fresh, preferred_element_type=jnp.float32) * SCORE_SCALE
    )
    row_step = (row_start + jnp.arange(own, dtype=jnp.int32)) // HEADS
    col_step = jnp.arange(fresh.shape[1], dtype=jnp.int32)
    scores = jnp.where((col_step[None, :] <= row_step[:, None])[None], scores, NEG_FILL)
    return pl.pallas_call(
        finish_kernel,
        out_shape=jax.ShapeDtypeStruct((4, own, LATENT_CHANNELS), jnp.bfloat16),
        in_specs=[VMEM] * 3,
        out_specs=VMEM,
        compiler_params=params(),
        cost_estimate=pl.CostEstimate(flops=0, bytes_accessed=1 << 20, transcendentals=0),
        name="finish",
    )(scores, fresh, joined)


def tie(*xs):
    return lax.optimization_barrier(xs)


def over_seq(x):
    return lax.all_to_all(x, "seq", split_axis=0, concat_axis=0, tiled=True)


def all_along(x):
    return lax.all_to_all(x, "grp", split_axis=0, concat_axis=0, tiled=True)


def along(x, d):
    return lax.ppermute(x, "grp", [(i, (i + d) % 4) for i in range(4)])


def local(
    compressed,
    block_channel_scale,
    outlier_channels,
    outlier_values,
    lengths,
    assignment,
    padding,
    queries,
    decode_token_latent,
):
    group_here = lax.axis_index("grp")
    seq_here = lax.axis_index("seq")
    rows_here = [lax.dynamic_index_in_dim(x, group_here, 0, keepdims=False) for x in (lengths, assignment, padding)]
    place = jnp.stack([group_here, seq_here]).astype(jnp.int32)
    table = jnp.concatenate([place] + rows_here)
    packed = compressed.T
    channels = outlier_channels.T

    starts = [sum(CHUNKS[:i]) for i in range(len(CHUNKS))]
    last = len(CHUNKS) - 1
    latent = [
        dequantize(start, rows, lengths, padding, packed, block_channel_scale, channels, outlier_values)
        for start, rows in zip(starts, CHUNKS)
    ]
    turned = queries.transpose(0, 2, 1)
    latent[0], turned = tie(latent[0], turned)
    pieces = [along(x, d) for d, x in zip((1, 2, 3), split(table, turned))]
    handed = hand(table, turned, pieces)
    handed = lax.ppermute(handed, "seq", [(j, j ^ 1) for j in range(32)])

    stripes, latent[1], handed, *pieces = tie(over_seq(latent[0]), latent[1], handed, *pieces)

    one, two, three, cache = pack(starts[0], table, stripes, None)
    following, one, two, three = tie(latent[1], one, two, three)
    one, two, three = along(one, 1), along(two, 2), along(three, 3)
    partial = attend(table, turned, pieces, handed, latent)
    stripes, partial, *first = tie(over_seq(following), partial, one, two, three)

    one, two, three, cache = pack(starts[1], table, stripes, cache)
    partial, cache, one, two, three = tie(partial, cache, one, two, three)
    one, two, three = along(one, 1), along(two, 2), along(three, 3)
    cache = put(starts[0], table, (1, 2, 3), first, cache, later=True, cost=LONG)
    following, cache = tie(partial.reshape(32, 16, -1), cache)
    joined = all_along(join(table, over_seq(following)))
    cache = put(starts[1], table, (2,), (two,), cache)
    cache = put(starts[1], table, (1, 3), (one, three), cache)
    joined, cache = tie(joined, cache)
    attended = finish(joined, queries, decode_token_latent, seq_here)
    return cache.transpose(0, 1, 3, 2)[None, :, None], attended


def solution(mesh):
    placed = (
        P(("grp", "seq"), None),
        P(("grp", "seq"), None),
        P(("grp", "seq"), None),
        P(("grp", "seq"), None, None),
        P(),
        P(),
        P(),
        P("grp", None, None),
        P("grp", None, None),
    )
    return jax.shard_map(
        local,
        mesh=mesh,
        in_specs=placed,
        out_specs=(P("grp", None, "seq", None, None, None), P("grp", "seq", None)),
        check_vma=False,
    )
```

```python
import functools

import jax
import jax.numpy as jnp
from jax import lax
from jax.experimental import pallas as pl
from jax.experimental.pallas import tpu as pltpu
from jax.sharding import PartitionSpec as P

LATENT_CHANNELS = 512
MOST_STRIPES = 12
HEADS = 128
NEG_FILL = -1e30
SCORE_SCALE = 192.0 ** (-0.5)
CHUNKS = (288, 288)
KEY_TILE = 16
KEY_PART = 4
NOTE_LANES = 128

SMEM = pl.BlockSpec(memory_space=pltpu.SMEM)
HBM = pl.BlockSpec(memory_space=pltpu.HBM)
VMEM = pl.BlockSpec(memory_space=pltpu.VMEM)


LONG = pl.CostEstimate(flops=40 << 30, bytes_accessed=0, transcendentals=0)


def params(megabytes=16):
    return pltpu.CompilerParams(vmem_limit_bytes=megabytes << 20)


def moved(steps, rows):
    size = 2 * steps * MOST_STRIPES * rows * 128
    return pl.CostEstimate(flops=0, bytes_accessed=2 * size, transcendentals=0)


def request_for(table, target):
    first, count, before = 0, 0, 0
    for r in range(4):
        here = table[2 + r]
        hit = table[6 + r] == target
        first = jnp.where(hit, before, first)
        count = jnp.where(hit, here, count)
        before = before + here
    return first, count


def request_of(table, stripe):
    target, empty, before = 0, 0, 0
    for r in range(4):
        after = before + table[2 + r]
        inside = jnp.logical_and(stripe >= before, stripe < after)
        target = jnp.where(inside, table[6 + r], target)
        empty = jnp.where(stripe == after - 1, table[10 + r], empty)
        before = after
    return target, empty


def dequantize_kernel(start, per_step, total, lengths, padding, packed, scale, channels, values, out, scales, marks):
    rows = packed.shape[0]
    width = per_step * 16
    step = pl.program_id(0)

    @pl.when(step == 0)
    def _():
        mark = channels[...].astype(jnp.float32).T
        low, high = start // 128 * 128, min(-(-(start + rows) // 128) * 128, scale.shape[1])
        plain = scale[:, low:high]
        ids = (lax.broadcasted_iota(jnp.int32, plain.shape, 1) + low).astype(jnp.float32)
        for k in range(16):
            plain = jnp.where(ids == mark[:, k : k + 1], 0.0, plain)
        turned = plain.T[start - low : start - low + rows]
        for i in range(total):
            scales[i] = turned[:, i * per_step : (i + 1) * per_step]
            marks[i] = jnp.concatenate([mark[i * per_step + b : i * per_step + b + 1] for b in range(per_step)], axis=1)

    group, stripe = lax.axis_index("grp"), lax.axis_index("seq")
    empty, before = 0, 0
    for r in range(4):
        before = before + lengths[group, r]
        empty = jnp.where(stripe == before - 1, padding[group, r], empty)
    ids = (lax.broadcasted_iota(jnp.int32, (rows, width), 0) + start).astype(jnp.float32)
    onehot = (ids == marks[step]).astype(jnp.bfloat16)
    flat = values[...].reshape(width, 128)
    block = lax.broadcasted_iota(jnp.int32, (width, 128), 0) // 16
    spread = jnp.concatenate([jnp.where(block == b, flat, jnp.zeros_like(flat)) for b in range(per_step)], axis=1)
    outliers = jnp.dot(onehot, spread, preferred_element_type=jnp.float32)
    tokens = lax.broadcasted_iota(jnp.int32, (rows, 128), 1)
    here = scales[step]
    for b in range(per_step):
        lanes = slice(b * 128, (b + 1) * 128)
        latent = packed[:, lanes].astype(jnp.float32) * here[:, b : b + 1] + outliers[:, lanes]
        if b == per_step - 1:
            limit = jnp.where(step == total - 1, 128 - empty, 128)
            latent = jnp.where(tokens < limit, latent, 0.0)
        out[b] = latent.astype(jnp.bfloat16)


def dequantize(start, rows, lengths, padding, packed, scale, channels, values):
    packed, values = [pltpu.with_memory_space_constraint(x, pltpu.HBM) for x in (packed, values)]
    blocks = scale.shape[0]
    per_step = 16
    steps = blocks // per_step
    return pl.pallas_call(
        functools.partial(dequantize_kernel, start, per_step, steps),
        grid=(steps,),
        out_shape=pltpu.HBM((blocks, rows, 128), jnp.bfloat16),
        in_specs=[
            SMEM,
            SMEM,
            pl.BlockSpec((pl.Element(rows), pl.Element(per_step * 128)), lambda i: (start, i * per_step * 128)),
            pl.BlockSpec(scale.shape, lambda i: (0, 0)),
            pl.BlockSpec(channels.shape, lambda i: (0, 0)),
            pl.BlockSpec((per_step, 16, 128), lambda i: (i, 0, 0)),
        ],
        out_specs=pl.BlockSpec((per_step, rows, 128), lambda i: (i, 0, 0)),
        scratch_shapes=[
            pltpu.VMEM((steps, rows, per_step), jnp.float32),
            pltpu.VMEM((steps, 1, per_step * 16), jnp.float32),
        ],
        compiler_params=params(60),
        cost_estimate=pl.CostEstimate(flops=0, bytes_accessed=4 * blocks * rows * 128, transcendentals=0),
        name="dequantize",
    )(lengths, padding, packed, scale, channels, values)


def collect(table, d, stripes, target, zeros, sem):
    first, count = request_for(table, lax.rem(table[0] + d, 4))
    for v in range(MOST_STRIPES):

        @pl.when(v < count)
        def _():
            pltpu.make_async_copy(stripes.at[first + v], target.at[v], sem).start()

        @pl.when(v >= count)
        def _():
            pltpu.make_async_copy(zeros, target.at[v], sem).start()


def pack_kernel(start, table, stripes, *refs):
    *outs, cache, zeros, sems = refs[-6:]
    zeros[...] = jnp.zeros_like(zeros)
    targets = [cache.at[table[0], :, pl.ds(start, stripes.shape[1]), :], *outs]
    for d in (2, 1, 3, 0):
        collect(table, d, stripes, targets[d], zeros, sems.at[d])
    for d, target in enumerate(targets):
        pltpu.make_async_copy(target, target, sems.at[d]).wait()


def pack(start, table, stripes, cache):
    rows = stripes.shape[1]
    more = () if cache is None else (cache,)
    one = pltpu.HBM((MOST_STRIPES, rows, 128), jnp.bfloat16)
    return pl.pallas_call(
        functools.partial(pack_kernel, start),
        out_shape=(one, one, one, jax.ShapeDtypeStruct((4, MOST_STRIPES, sum(CHUNKS), 128), jnp.bfloat16)),
        in_specs=[SMEM, VMEM] + [HBM] * len(more),
        out_specs=(HBM,) * 4,
        input_output_aliases={2: 3} if more else {},
        scratch_shapes=[pltpu.VMEM((rows, 128), jnp.bfloat16), pltpu.SemaphoreType.DMA((4,))],
        compiler_params=params(),
        cost_estimate=moved(4, rows),
        name="pack",
    )(table, stripes, *more)


PIECES = 3


def put_copies(start, steps, table, arrived, out, sems):
    rows, size = arrived[0].shape[1], MOST_STRIPES // PIECES
    copies = []
    for i, d in enumerate(steps):
        slot = out.at[lax.rem(table[0] + 4 - d, 4)]
        for h in range(PIECES):
            part = pl.ds(h * size, size)
            copies.append(
                pltpu.make_async_copy(arrived[i].at[part], slot.at[part, pl.ds(start, rows), :], sems.at[i, h])
            )
    return copies


def put_kernel(start, steps, table, *refs):
    arrived, (out, sems) = refs[: len(steps)], refs[-2:]
    copies = put_copies(start, steps, table, arrived, out, sems)
    for copy in copies:
        copy.start()
    for copy in copies:
        copy.wait()


def put_later_kernel(start, steps, table, *refs):
    arrived, (out, sems, held, in_sems) = refs[: len(steps)], refs[-4:]
    come = [pltpu.make_async_copy(arrived[i], held.at[i], in_sems.at[i]) for i in range(len(steps))]
    leave = put_copies(start, steps, table, [held.at[i] for i in range(len(steps))], out, sems)
    for copy in come:
        copy.start()
    for i, copy in enumerate(come):
        copy.wait()
        for part in leave[i * PIECES : (i + 1) * PIECES]:
            part.start()
    for part in leave:
        part.wait()


def put(start, table, steps, arrived, cache, later=False, cost=None):
    rows = arrived[0].shape[1]
    scratch = [pltpu.SemaphoreType.DMA((len(steps), PIECES))]
    if later:
        scratch += [
            pltpu.VMEM((len(steps), MOST_STRIPES, rows, 128), jnp.bfloat16),
            pltpu.SemaphoreType.DMA((len(steps),)),
        ]
    return pl.pallas_call(
        functools.partial(put_later_kernel if later else put_kernel, start, steps),
        out_shape=jax.ShapeDtypeStruct((4, MOST_STRIPES, sum(CHUNKS), 128), jnp.bfloat16),
        in_specs=[SMEM] + [pl.BlockSpec(memory_space=pl.ANY) if later else VMEM] * len(steps) + [HBM],
        out_specs=HBM,
        input_output_aliases={len(steps) + 1: 0},
        scratch_shapes=scratch,
        compiler_params=params(),
        cost_estimate=cost or moved(len(steps), rows),
        name="put",
    )(table, *arrived, cache)


def partner(table):
    return table[1] + 1 - 2 * lax.rem(table[1], 2)


def half_of(table, rows):
    return pl.ds(pl.multiple_of(lax.rem(table[1], 2) * rows, rows), rows)


def split_kernel(table, queries, *refs):
    outs, (held, in_sems, out_sems) = refs[:3], refs[3:]
    half = half_of(table, held.shape[1])
    come = [
        pltpu.make_async_copy(queries.at[lax.rem(table[0] + d + 1, 4), half], held.at[d], in_sems.at[d])
        for d in range(3)
    ]
    leave = [pltpu.make_async_copy(held.at[d], outs[d], out_sems.at[d]) for d in range(3)]
    for copy in come:
        copy.start()
    for d in range(3):
        come[d].wait()
        leave[d].start()
    for copy in leave:
        copy.wait()


def split(table, queries):
    shape = (queries.shape[1] // 2, queries.shape[2])
    return pl.pallas_call(
        split_kernel,
        out_shape=(pltpu.HBM(shape, queries.dtype),) * 3,
        in_specs=[SMEM, HBM],
        out_specs=(HBM,) * 3,
        scratch_shapes=[
            pltpu.VMEM((3,) + shape, queries.dtype),
            pltpu.SemaphoreType.DMA((3,)),
            pltpu.SemaphoreType.DMA((3,)),
        ],
        compiler_params=params(),
        cost_estimate=pl.CostEstimate(flops=0, bytes_accessed=1 << 20, transcendentals=0),
        name="split",
    )(table, pltpu.with_memory_space_constraint(queries, pltpu.HBM))


def start_half(table, target, queries, pieces, out, sem):
    for d in range(4):
        source = queries.at[table[0], half_of(table, out.shape[0])] if d == 0 else pieces[d - 1]

        @pl.when(target == lax.rem(table[0] + 4 - d, 4))
        def _():
            pltpu.make_async_copy(source, out, sem).start()


def hand_kernel(table, queries, in1, in2, in3, out, sem):
    target, _ = request_of(table, partner(table))
    start_half(table, target, queries, (in1, in2, in3), out, sem)
    pltpu.make_async_copy(in1, out, sem).wait()


def hand(table, queries, pieces):
    queries = pltpu.with_memory_space_constraint(queries, pltpu.HBM)
    return pl.pallas_call(
        hand_kernel,
        out_shape=jax.ShapeDtypeStruct(pieces[0].shape, pieces[0].dtype),
        in_specs=[SMEM, HBM] + [VMEM] * 3,
        out_specs=VMEM,
        scratch_shapes=[pltpu.SemaphoreType.DMA],
        compiler_params=params(),
        cost_estimate=pl.CostEstimate(flops=0, bytes_accessed=1 << 20, transcendentals=0),
        name="hand",
    )(table, queries, *pieces)


def in_three(x):
    high = x.astype(jnp.bfloat16)
    rest = x - high.astype(jnp.float32)
    middle = rest.astype(jnp.bfloat16)
    low = (rest - middle.astype(jnp.float32)).astype(jnp.bfloat16)
    return high, middle, low


def attend_kernel(steps, table, *refs):
    sources, handed, keys = refs[:4], refs[4], refs[5 : 5 + len(CHUNKS)]
    out, peak, total, weighted, turned, queries, sems = refs[5 + len(CHUNKS) :]
    step = pl.program_id(0)
    target, empty = request_of(table, table[1])

    @pl.when(step == 0)
    def _():
        rows = handed.shape[0]
        mine, other = turned.at[half_of(table, rows)], turned.at[half_of((0, partner(table)), rows)]
        start_half(table, target, sources[0], sources[1:], mine, sems.at[0])
        copy = pltpu.make_async_copy(handed, other, sems.at[1])
        copy.start()
        copy.wait()
        pltpu.make_async_copy(sources[1], mine, sems.at[0]).wait()
        queries[...] = turned[...].T
        peak[...] = jnp.full_like(peak, NEG_FILL)
        total[...] = jnp.zeros_like(total)
        weighted[...] = jnp.zeros_like(weighted)

    parts = [
        jnp.concatenate(
            [jnp.concatenate([k[b] for k in keys], axis=0) for b in range(i, i + KEY_PART)], axis=1
        )
        for i in range(0, KEY_TILE, KEY_PART)
    ]
    scores = [jnp.dot(queries[...], part, preferred_element_type=jnp.float32) for part in parts]
    limit = jnp.where(step == steps - 1, KEY_PART * 128 - empty, KEY_PART * 128)
    columns = lax.broadcasted_iota(jnp.int32, (1, KEY_PART * 128), 1)
    scores[-1] = scores[-1] + jnp.where(columns < limit, 0.0, NEG_FILL)
    before = peak[...]
    now = before
    for score in scores:
        now = jnp.maximum(now, jnp.max(score, axis=1, keepdims=True))
    shrink = jnp.exp((before - now) * SCORE_SCALE)
    whole, sums = total[...] * shrink, weighted[...] * shrink[:, :1]
    for score, part in zip(scores, parts):
        weights = jnp.exp((score - now[:, :1]) * SCORE_SCALE).astype(jnp.bfloat16)
        whole = whole + jnp.sum(weights.astype(jnp.float32), axis=1, keepdims=True)
        sums = sums + lax.dot_general(
            weights, part[:LATENT_CHANNELS], (((1,), (1,)), ((), ())), preferred_element_type=jnp.float32
        )
    total[...], weighted[...], peak[...] = whole, sums, now

    @pl.when(step == steps - 1)
    def _():
        out[:, :LATENT_CHANNELS] = weighted[...].astype(jnp.bfloat16)
        lane = lax.broadcasted_iota(jnp.int32, peak.shape, 1)
        note = jnp.zeros(peak.shape, jnp.float32)
        for i, part in enumerate(in_three(peak[...] * SCORE_SCALE) + in_three(total[...])):
            note = jnp.where(lane == i, part.astype(jnp.float32), note)
        out[:, LATENT_CHANNELS:] = note.astype(jnp.bfloat16)


def attend(table, queries, pieces, handed, keys):
    channels, rows = queries.shape[1:]
    queries = pltpu.with_memory_space_constraint(queries, pltpu.HBM)
    keys = [pltpu.with_memory_space_constraint(k, pltpu.HBM) for k in keys]
    blocks = keys[0].shape[0]
    steps = blocks // KEY_TILE
    width = LATENT_CHANNELS + NOTE_LANES
    return pl.pallas_call(
        functools.partial(attend_kernel, steps),
        grid=(steps,),
        out_shape=pltpu.HBM((rows, width), jnp.bfloat16),
        in_specs=[SMEM, HBM] + [VMEM] * 4
        + [pl.BlockSpec((KEY_TILE,) + k.shape[1:], lambda i: (i, 0, 0)) for k in keys],
        out_specs=pl.BlockSpec((rows, width), lambda i: (0, 0)),
        scratch_shapes=[
            pltpu.VMEM((rows, 128), jnp.float32),
            pltpu.VMEM((rows, 128), jnp.float32),
            pltpu.VMEM((rows, LATENT_CHANNELS), jnp.float32),
            pltpu.VMEM((channels, rows), jnp.bfloat16),
            pltpu.VMEM((rows, channels), jnp.bfloat16),
            pltpu.SemaphoreType.DMA((2,)),
        ],
        compiler_params=params(44),
        cost_estimate=LONG,
        name="attend",
    )(table, queries, *pieces, handed, *keys)


def join_kernel(table, partials, out):
    stripes, rows, _ = partials.shape
    note = partials[:, :, LATENT_CHANNELS:].astype(jnp.float32)
    peak = note[:, :, 0:1] + note[:, :, 1:2] + note[:, :, 2:3]
    total = note[:, :, 3:4] + note[:, :, 4:5] + note[:, :, 5:6]
    stripe = lax.broadcasted_iota(jnp.int32, peak.shape, 0)
    lane = lax.broadcasted_iota(jnp.int32, (rows, NOTE_LANES), 1)
    values = partials[:, :, :LATENT_CHANNELS].astype(jnp.float32)
    for d in range(4):
        first, count = request_for(table, d)
        inside = jnp.logical_and(stripe >= first, stripe < first + count)
        top = jnp.max(jnp.where(inside, peak, NEG_FILL), axis=0)
        factor = jnp.where(inside, jnp.exp(jnp.where(inside, peak, NEG_FILL) - top[None]), 0.0)
        out[d, :, :LATENT_CHANNELS] = jnp.sum(values * factor, axis=0)
        whole = jnp.sum(total * factor, axis=0)
        out[d, :, LATENT_CHANNELS:] = jnp.where(lane == 0, top, jnp.where(lane == 1, whole, 0.0))


def join(table, partials):
    return pl.pallas_call(
        join_kernel,
        out_shape=jax.ShapeDtypeStruct((4,) + partials.shape[1:], jnp.float32),
        in_specs=[SMEM, VMEM],
        out_specs=VMEM,
        compiler_params=params(),
        cost_estimate=pl.CostEstimate(flops=0, bytes_accessed=1 << 20, transcendentals=0),
        name="join",
    )(table, partials)


def finish_kernel(scores, fresh, joined, out):
    for slot in range(4):
        cache_peak = joined[slot, :, LATENT_CHANNELS : LATENT_CHANNELS + 1]
        cache_total = joined[slot, :, LATENT_CHANNELS + 1 : LATENT_CHANNELS + 2]
        peak = jnp.maximum(cache_peak, jnp.max(scores[slot], axis=1, keepdims=True))
        shrink = jnp.exp(cache_peak - peak)
        weights = jnp.exp(scores[slot] - peak).astype(jnp.bfloat16)
        weighted = joined[slot, :, :LATENT_CHANNELS] * shrink + jnp.dot(
            weights, fresh[slot][:, :LATENT_CHANNELS], preferred_element_type=jnp.float32
        )
        total = cache_total * shrink + jnp.sum(weights.astype(jnp.float32), axis=1, keepdims=True)
        out[slot] = (weighted / total).astype(jnp.bfloat16)


def finish(joined, queries, fresh, seq_here):
    own = joined.shape[1]
    row_start = seq_here * own
    own_queries = lax.dynamic_slice_in_dim(queries, row_start, own, 1)
    scores = (
        jnp.einsum("yeu,ynu->yen", own_queries, fresh, preferred_element_type=jnp.float32) * SCORE_SCALE
    )
    row_step = (row_start + jnp.arange(own, dtype=jnp.int32)) // HEADS
    col_step = jnp.arange(fresh.shape[1], dtype=jnp.int32)
    scores = jnp.where((col_step[None, :] <= row_step[:, None])[None], scores, NEG_FILL)
    return pl.pallas_call(
        finish_kernel,
        out_shape=jax.ShapeDtypeStruct((4, own, LATENT_CHANNELS), jnp.bfloat16),
        in_specs=[VMEM] * 3,
        out_specs=VMEM,
        compiler_params=params(),
        cost_estimate=pl.CostEstimate(flops=0, bytes_accessed=1 << 20, transcendentals=0),
        name="finish",
    )(scores, fresh, joined)


def tie(*xs):
    return lax.optimization_barrier(xs)


def over_seq(x):
    return lax.all_to_all(x, "seq", split_axis=0, concat_axis=0, tiled=True)


def all_along(x):
    return lax.all_to_all(x, "grp", split_axis=0, concat_axis=0, tiled=True)


def along(x, d):
    return lax.ppermute(x, "grp", [(i, (i + d) % 4) for i in range(4)])


def local(
    compressed,
    block_channel_scale,
    outlier_channels,
    outlier_values,
    lengths,
    assignment,
    padding,
    queries,
    decode_token_latent,
):
    group_here = lax.axis_index("grp")
    seq_here = lax.axis_index("seq")
    rows_here = [lax.dynamic_index_in_dim(x, group_here, 0, keepdims=False) for x in (lengths, assignment, padding)]
    place = jnp.stack([group_here, seq_here]).astype(jnp.int32)
    table = jnp.concatenate([place] + rows_here)
    packed = compressed.T
    channels = outlier_channels.T

    starts = [sum(CHUNKS[:i]) for i in range(len(CHUNKS))]
    last = len(CHUNKS) - 1
    latent = [
        dequantize(start, rows, lengths, padding, packed, block_channel_scale, channels, outlier_values)
        for start, rows in zip(starts, CHUNKS)
    ]
    turned = queries.transpose(0, 2, 1)
    latent[0], turned = tie(latent[0], turned)
    pieces = [along(x, d) for d, x in zip((1, 2, 3), split(table, turned))]
    handed = hand(table, turned, pieces)
    handed = lax.ppermute(handed, "seq", [(j, j ^ 1) for j in range(32)])

    stripes, latent[1], handed, *pieces = tie(over_seq(latent[0]), latent[1], handed, *pieces)

    one, two, three, cache = pack(starts[0], table, stripes, None)
    following, one, two, three = tie(latent[1], one, two, three)
    one, two, three = along(one, 1), along(two, 2), along(three, 3)
    partial = attend(table, turned, pieces, handed, latent)
    stripes, partial, *first = tie(over_seq(following), partial, one, two, three)

    one, two, three, cache = pack(starts[1], table, stripes, cache)
    partial, cache, one, two, three = tie(partial, cache, one, two, three)
    one, two, three = along(one, 1), along(two, 2), along(three, 3)
    cache = put(starts[0], table, (1, 2, 3), first, cache, later=True, cost=LONG)
    following, cache = tie(partial.reshape(32, 16, -1), cache)
    joined = all_along(join(table, over_seq(following)))
    cache = put(starts[1], table, (2,), (two,), cache)
    cache = put(starts[1], table, (1, 3), (one, three), cache)
    joined, cache = tie(joined, cache)
    attended = finish(joined, queries, decode_token_latent, seq_here)
    return cache.transpose(0, 1, 3, 2)[None, :, None], attended


def solution(mesh):
    placed = (
        P(("grp", "seq"), None),
        P(("grp", "seq"), None),
        P(("grp", "seq"), None),
        P(("grp", "seq"), None, None),
        P(),
        P(),
        P(),
        P("grp", None, None),
        P("grp", None, None),
    )
    return jax.shard_map(
        local,
        mesh=mesh,
        in_specs=placed,
        out_specs=(P("grp", None, "seq", None, None, None), P("grp", "seq", None)),
        check_vma=False,
    )
```
